128 devices in a mesh: sp: 8 (over z, core), ep: 16 (over x, y).
Axes of the slice: x: 4, y: 4, z: 4, core: 2. Of those that a mesh axis runs over, the one named last changes fastest.
Arguments:
- hidden_in: bfloat16 [16, 1024, 4096], P('ep', 'sp'), may hold values from -6 to 6
- queries: bfloat16 [16, 1024, 4096], P('ep', 'sp'), may hold values from -160 to 160
- keys: bfloat16 [16, 1024, 256], P('ep', 'sp'), may hold values from -5 to 5
- values: bfloat16 [16, 1024, 256], P('ep', 'sp'), may hold values from -6 to 6
- out_weight: bfloat16 [4096, 4096], P('sp', 'ep'), may hold values from -0.09375 to 0.09375
- norm_gain: float32 [4096], replicated, may hold values from 0.25 to 1.75
- gate_weight: bfloat16 [128, 4096, 768], P(('sp', 'ep')), may hold values from -0.09375 to 0.09375
- up_weight: bfloat16 [128, 4096, 768], P(('sp', 'ep')), may hold values from -0.09375 to 0.09375
- down_weight: bfloat16 [128, 768, 4096], P(('sp', 'ep')), may hold values from -0.21875 to 0.21875
- expert_ids: int32 [16, 1024, 8], P('ep', 'sp'), may hold values from 0 to 127, all different within a row; in each aligned block of 128 rows (0 to 127, 128 to 255, ..., all dimensions but the last counted through in order) at most 9 rows name the same one
- gates: float32 [16, 1024, 8], P('ep', 'sp'), may hold values from 0.05 to 0.4
- cotangent: bfloat16 [16, 1024, 4096], P('ep', 'sp'), may hold values from -0.25 to 0.25
Outputs:
- layer_out: bfloat16 [16, 1024, 4096], P('ep', 'sp')
- gate_grad: float32 [16, 1024, 8], P('ep', 'sp')
The draws below stay inside these ranges and needn't reach their ends.
Inputs may be any that keep to these rules, and one draw needn't show every extreme that they name: `expert_ids`: in the rows of one device (aligned blocks of 128 rows) no expert is named by more than 9 rows, a bound that some block reaches.
All inputs are finite; a program needn't handle non-finite values.
Results may differ from the reference program's by a relative error of at most 0.023.
Values may be sent and summed in bfloat16 or wider, within the bound.
A program may use at most 128 MiB of HBM per device.

```python
import math
import jax
import jax.numpy as jnp
import numpy as np
from jax import lax

D = 4096
QUERY_HEAD_COUNT = 32
KEY_VALUE_HEADS = 2
HEAD_SIZE = 128
FFW = 768
TOP = 8
TOK_DEV = 128
SLAB_POSITIONS = 1024
SLAB_COUNT = 16
TOKENS = 16384
EXPERTS = 128
CAP = 9
N_SP = 8
N_EP = 16


def shared_keys(key):
    return jnp.clip(jax.random.normal(key, (SLAB_COUNT, SLAB_POSITIONS, KEY_VALUE_HEADS * HEAD_SIZE), jnp.float32), -4.5, 4.5)


def draw_keys(key, part):
    start_offset = shared_keys(key)
    return start_offset.astype(jnp.bfloat16)


def draw_queries(key, part):
    key = jax.random.fold_in(key, 3)
    query = jnp.clip(jax.random.normal(key, (SLAB_COUNT, SLAB_POSITIONS, QUERY_HEAD_COUNT * HEAD_SIZE), jnp.float32), -4.5, 4.5)
    return query.astype(jnp.bfloat16)


def steps_of(stream_key, dims, cuts, least, high):
    level, own = 1.0, jax.random.fold_in(stream_key, 6)
    for dim, blocks in cuts:
        steps = jnp.exp(jax.random.uniform(jax.random.fold_in(own, dim), (blocks,), jnp.float32, least / len(cuts), high / len(cuts)))
        level = level * jnp.repeat(steps, dims[dim] // blocks).reshape([-1 if axis == dim else 1 for axis in range(len(dims))])
    return level


def deal_out(key, own, number, rows, count, top, most, lean):
    order = jax.random.permutation(key, count)
    packed, usual = shares(count, rows * top, most, lean, True), shares(count, rows * top, most, lean, False)
    places = jnp.arange(count)

    def named(sizes, turn):
        used = int((sizes > 0).sum())
        fixed = max(1, used // 4)
        passed = fixed + (places - fixed + turn * (used - fixed)) % max(1, count - fixed)
        return jnp.zeros((count,), jnp.int32).at[order[jnp.where(places < fixed, places, passed)]].set(jnp.asarray(sizes, jnp.int32))

    sizes = jnp.where(number % 4 == 0, named(packed, number // 4), named(usual, number - number // 4 - 1))
    mixed = jax.random.permutation(jax.random.fold_in(own, 3), count)
    giver, sink = mixed[0:count // 2 * 2:2], mixed[1:count // 2 * 2:2]
    slack = jnp.minimum(sizes[giver] - 1, most - sizes[sink]) // 2
    slack = jnp.where((giver == order[0]) | (sink == order[0]) | (sizes[sink] == 0), 0, jnp.maximum(slack, 0))
    passed = jax.random.randint(jax.random.fold_in(own, 4), (count // 2,), 0, 1 << 20) % (slack + 1)
    sizes = sizes.at[giver].add(-passed).at[sink].add(passed)
    items = jnp.searchsorted(jnp.cumsum(sizes), jnp.arange(rows * top), side="right").astype(jnp.int32)
    grid = items.reshape(top, rows).T
    grid = grid[jax.random.permutation(jax.random.fold_in(own, 1), rows)]
    turn = jax.random.randint(jax.random.fold_in(own, 2), (rows, 1), 0, top)
    return jnp.take_along_axis(grid, (jnp.arange(top)[None, :] + turn) % top, axis=1)


def shares(number_of, total, reach, lean, full):
    portions = [(1 << 20) // math.isqrt(grade ** lean) + 1 for grade in range(1, number_of + 1)]
    largest = reach if full else min(reach, max(-(-total // number_of), total * portions[0] // sum(portions)))
    least = 1 if total - largest >= number_of - 1 else 0
    holding, spare = [largest] + [least] * (number_of - 1), total - largest - least * (number_of - 1)
    while spare > 0:
        candidates = [i for i in range(1, number_of) if holding[i] < largest] or [i for i in range(1, number_of) if holding[i] < reach]
        pool, budget = sum([portions[i] for i in candidates]), spare
        for i in candidates:
            addition = min(reach - holding[i], max(1, budget * portions[i] // pool), spare)
            holding[i] = holding[i] + addition
            spare = spare - addition
    return np.array(holding)


def bell_draw(key, dims, scale, limit, split=(), kind=jnp.bfloat16):
    values = scale * jax.random.normal(key, dims, jnp.float32)
    if split:
        values = values * steps_of(key, dims, split, -0.22, 0.18)
    return jnp.clip(values, -limit, limit).astype(kind)


def setup_inputs(seed: int = 0) -> dict:
    streams_of = jax.random.split(jax.random.key(seed), 13)
    hidden_in = bell_draw(streams_of[0], (SLAB_COUNT, SLAB_POSITIONS, D), 1.0, 6.0, ((0, 16), (1, 8)))
    queries = draw_queries(jax.random.fold_in(streams_of[12], 71), 0)
    keys = draw_keys(jax.random.fold_in(streams_of[12], 71), 0)
    values = bell_draw(streams_of[3], (SLAB_COUNT, SLAB_POSITIONS, KEY_VALUE_HEADS * HEAD_SIZE), 1.0, 6.0, ((0, 16), (1, 8)))
    out_weight = bell_draw(streams_of[4], (QUERY_HEAD_COUNT * HEAD_SIZE, D), (QUERY_HEAD_COUNT * HEAD_SIZE) ** -0.5, 0.09375, ((0, 8), (1, 16)))
    norm_gain = jnp.clip(1.0 + 0.15 * jax.random.normal(streams_of[5], (D,), jnp.float32), 0.25, 1.75)
    gate_weight = bell_draw(streams_of[6], (EXPERTS, D, FFW), D ** -0.5, 0.09375, ((0, 128),))
    up_weight = bell_draw(streams_of[7], (EXPERTS, D, FFW), D ** -0.5, 0.09375, ((0, 128),))
    down_weight = bell_draw(streams_of[8], (EXPERTS, FFW, D), FFW ** -0.5, 0.21875, ((0, 128),))
    expert_ids_keys = jax.random.split(jax.random.fold_in(streams_of[9], 1), SLAB_COUNT * SLAB_POSITIONS // TOK_DEV)
    expert_ids_turns = jax.random.permutation(jax.random.fold_in(streams_of[9], 3), SLAB_COUNT * SLAB_POSITIONS // TOK_DEV)
    expert_ids = jax.vmap(lambda own, number: deal_out(jax.random.fold_in(streams_of[9], 2), own, number, TOK_DEV, EXPERTS, TOP, CAP, 2))(expert_ids_keys, expert_ids_turns).reshape((SLAB_COUNT, SLAB_POSITIONS, TOP))
    gates = jnp.clip(jnp.exp(math.log(0.4) - 2.0794415 * jax.random.uniform(streams_of[10], (SLAB_COUNT, SLAB_POSITIONS, TOP), jnp.float32) ** steps_of(streams_of[10], (SLAB_COUNT, SLAB_POSITIONS, TOP), ((0, 16), (1, 8)), -0.2, 0.2)), 0.05, 0.4)
    cotangent = bell_draw(streams_of[11], (SLAB_COUNT, SLAB_POSITIONS, D), 0.015625, 0.25, ((0, 16), (1, 8)))
    return {"hidden_in": hidden_in, "queries": queries, "keys": keys, "values": values, "out_weight": out_weight, "norm_gain": norm_gain, "gate_weight": gate_weight, "up_weight": up_weight, "down_weight": down_weight, "expert_ids": expert_ids, "gates": gates, "cotangent": cotangent}


def attend_slab(query_slab, slab_key_rows, slab_value_rows):
    query_group = QUERY_HEAD_COUNT // KEY_VALUE_HEADS
    head_lookup = jnp.arange(QUERY_HEAD_COUNT) // query_group
    q_three = query_slab.reshape(SLAB_POSITIONS, QUERY_HEAD_COUNT, HEAD_SIZE).astype(jnp.float32)
    key_triple = slab_key_rows.reshape(SLAB_POSITIONS, KEY_VALUE_HEADS, HEAD_SIZE).astype(jnp.float32)[:, head_lookup, :]
    value_triple = slab_value_rows.reshape(SLAB_POSITIONS, KEY_VALUE_HEADS, HEAD_SIZE).astype(jnp.float32)[:, head_lookup, :]
    scores = jnp.einsum('qhd,khd->hqk', q_three, key_triple) / jnp.sqrt(jnp.float32(HEAD_SIZE))
    rows = jnp.arange(SLAB_POSITIONS)[:, None]
    cols = jnp.arange(SLAB_POSITIONS)[None, :]
    scores = jnp.where((cols <= rows)[None], scores, jnp.float32(-1e+30))
    top = lax.optimization_barrier(jnp.max(scores, axis=-1, keepdims=True))
    expo = jnp.exp(scores - top)
    probs = (expo / lax.optimization_barrier(jnp.sum(expo, axis=-1, keepdims=True))).astype(jnp.bfloat16)
    out = jnp.einsum('hqk,khd->qhd', probs.astype(jnp.float32), value_triple)
    return out.astype(jnp.bfloat16).reshape(SLAB_POSITIONS, QUERY_HEAD_COUNT * HEAD_SIZE)

def mix_slab(attended, hidden_slab, out_weight):
    width = QUERY_HEAD_COUNT * HEAD_SIZE // N_SP
    total = hidden_slab.astype(jnp.float32)
    for group_index in range(N_SP):
        part = jnp.dot(attended[:, group_index * width:(group_index + 1) * width], out_weight[group_index * width:(group_index + 1) * width], preferred_element_type=jnp.float32).astype(jnp.bfloat16)
        part = lax.optimization_barrier(part)
        total = total + part.astype(jnp.float32)
    return total.astype(jnp.bfloat16)

def reference(hidden_in, queries, keys, values, out_weight, norm_gain, gate_weight, up_weight, down_weight, expert_ids, gates, cotangent):

    def one_slab(operands):
        query_slab, slab_key_rows, slab_value_rows, hidden_slab = operands
        return mix_slab(attend_slab(query_slab, slab_key_rows, slab_value_rows), hidden_slab, out_weight)
    mixed = lax.map(one_slab, (queries, keys, values, hidden_in))
    mixed_flat = mixed.reshape(TOKENS, D).astype(jnp.float32)
    scale = lax.rsqrt(lax.optimization_barrier(jnp.mean(mixed_flat * mixed_flat, axis=-1, keepdims=True)) + 1e-06)
    normed = (mixed_flat * scale * norm_gain).astype(jnp.bfloat16)
    blocks = expert_ids.reshape(SLAB_COUNT, N_SP, TOK_DEV * TOP)
    onehot = (blocks[..., None] == jnp.arange(EXPERTS, dtype=jnp.int32)).astype(jnp.int32)
    rank = jnp.cumsum(onehot, axis=2) - 1
    slot = lax.optimization_barrier(jnp.sum(rank * onehot, axis=-1))
    device = jnp.arange(N_SP, dtype=jnp.int32)[None, :] * N_EP + jnp.arange(SLAB_COUNT, dtype=jnp.int32)[:, None]
    position = blocks * (EXPERTS * CAP) + device[:, :, None] * CAP + slot
    position = position.reshape(-1).astype(jnp.int32)
    token_of = (jnp.arange(TOKENS * TOP, dtype=jnp.int32) // TOP).astype(jnp.int32)
    table = jnp.full((EXPERTS * EXPERTS * CAP,), TOKENS, jnp.int32).at[position].set(token_of)
    table = table.reshape(EXPERTS, EXPERTS * CAP)
    gate_table = jnp.zeros((EXPERTS * EXPERTS * CAP,), jnp.float32).at[position].set(gates.reshape(-1))
    gate_table = gate_table.reshape(EXPERTS, EXPERTS * CAP)
    normed_pad = jnp.concatenate([normed, jnp.zeros((1, D), jnp.bfloat16)], axis=0)
    cot_pad = jnp.concatenate([cotangent.reshape(TOKENS, D), jnp.zeros((1, D), jnp.bfloat16)], axis=0)

    def one_expert(acc, operands):
        rows, row_gates, w_gate, w_up, w_down = operands
        inputs = normed_pad[rows]
        gate_part = jnp.dot(inputs, w_gate, preferred_element_type=jnp.float32)
        up_part = jnp.dot(inputs, w_up, preferred_element_type=jnp.float32)
        inner = (jax.nn.silu(gate_part) * up_part).astype(jnp.bfloat16)
        out = jnp.dot(inner, w_down, preferred_element_type=jnp.float32).astype(jnp.bfloat16)
        out_f = out.astype(jnp.float32)
        acc = acc.at[rows].add(row_gates[:, None] * out_f)
        grads = lax.optimization_barrier(jnp.sum(cot_pad[rows].astype(jnp.float32) * out_f, axis=-1))
        return (acc, grads)
    start = jnp.zeros((TOKENS + 1, D), jnp.float32)
    acc, grad_table = lax.scan(one_expert, start, (table, gate_table, gate_weight, up_weight, down_weight))
    layer_out = (mixed_flat + acc[:TOKENS]).astype(jnp.bfloat16).reshape(SLAB_COUNT, SLAB_POSITIONS, D)
    gate_grad = grad_table.reshape(-1)[position].reshape(SLAB_COUNT, SLAB_POSITIONS, TOP)
    return (layer_out, gate_grad)
```

```python
import jax
import jax.numpy as jnp
import numpy as np
from jax import lax
from jax.experimental import pallas as pl
from jax.experimental.pallas import tpu as pltpu
from jax.sharding import PartitionSpec as P

D = 4096
QUERY_HEAD_COUNT = 32
KEY_VALUE_HEADS = 2
HEAD_SIZE = 128
TOP = 8


MESH = pl.DeviceIdType.MESH
CAP = 9
DEVICES = 128
ROWS = DEVICES * CAP
GROUPS = 4
GROUP_SLOTS = DEVICES // GROUPS
GROUP_ROWS = GROUP_SLOTS * CAP
FFW = 768
LANES = 128
FEATS = D // LANES


def offset_of(step):
    j = (step * (step + 1) // 2) % DEVICES
    return (j // 16) % 4, j // 64, (j // 4) % 4, j % 4


def place():
    sp, ep = lax.axis_index("sp"), lax.axis_index("ep")
    return sp // 2, sp % 2, ep // 4, ep % 4


def target_of(step):
    z, c, x, y = place()
    dz, dc, dx, dy = offset_of(step)
    turn = 1 - 2 * c
    return (
        ((z + turn * dz + 4) % 4) * 2 + (c + dc) % 2,
        ((x + turn * dx + 4) % 4) * 4 + (y + turn * dy + 4) % 4,
    )


def source_of(step):
    z, c, x, y = place()
    dz, dc, dx, dy = offset_of(step)
    core = (c + dc) % 2
    turn = 1 - 2 * core
    return (
        ((z - turn * dz + 4) % 4) * 2 + core,
        ((x - turn * dx + 4) % 4) * 4 + (y - turn * dy + 4) % 4,
    )


def chunk(step):
    return pl.ds(step * CAP, CAP)


def expert_kernel(
    token_ref,
    normed_ref,
    gate_hbm,
    up_hbm,
    down_hbm,
    back_ref,
    gate_w,
    up_w,
    down_w,
    send,
    recv,
    rows,
    inner,
    wide,
    weight_sem,
    send_sem,
    recv_sem,
    out_sem,
    back_sem,
):
    weights = [
        pltpu.make_async_copy(src, dst, weight_sem.at[i])
        for i, (src, dst) in enumerate(((gate_hbm, gate_w), (up_hbm, up_w), (down_hbm, down_w)))
    ]
    for copy in weights:
        copy.start()

    barrier = pltpu.get_barrier_semaphore()

    def greet(step, carry):
        pl.semaphore_signal(barrier, inc=1, device_id=target_of(step), device_id_type=MESH)
        return carry

    lax.fori_loop(1, DEVICES, greet, 0)

    def fill(step):
        for slot in range(CAP):
            row = step * CAP + slot
            send[row] = normed_ref[token_ref[row]]

    fill(0)
    pl.semaphore_wait(barrier, DEVICES - 1)
    pltpu.make_async_copy(send.at[chunk(0)], recv.at[chunk(0)], recv_sem.at[0]).start()

    def dispatch(step, carry):
        fill(step)
        pltpu.make_async_remote_copy(
            src_ref=send.at[chunk(step)],
            dst_ref=recv.at[chunk(step)],
            send_sem=send_sem,
            recv_sem=recv_sem.at[step // GROUP_SLOTS],
            device_id=target_of(step),
            device_id_type=MESH,
        ).start()
        return carry

    lax.fori_loop(1, DEVICES, dispatch, 0)
    for copy in weights:
        copy.wait()

    def work(group, carry):
        base = group * GROUP_ROWS
        block = pl.ds(base, GROUP_ROWS)
        pltpu.make_async_copy(recv.at[block], recv.at[block], recv_sem.at[group]).wait()

        def turn_in(i, carry):
            wide[pl.ds(0, 16 * FEATS), :] = (
                recv[pl.ds(base + i * 16, 16)].astype(jnp.float32).reshape(16 * FEATS, LANES)
            )
            for f in range(FEATS):
                rows[pl.ds(pl.multiple_of(i * 16, 16), 16), f * LANES : (f + 1) * LANES] = wide[
                    pl.ds(f, 16, stride=FEATS), :
                ].astype(jnp.bfloat16)
            return carry

        lax.fori_loop(0, GROUP_ROWS // 16, turn_in, 0)

        def hidden(n, carry):
            cols = pl.ds(pl.multiple_of(n * 256, 256), 256)
            gate_part = jnp.dot(rows[...], gate_w[:, cols], preferred_element_type=jnp.float32)
            up_part = jnp.dot(rows[...], up_w[:, cols], preferred_element_type=jnp.float32)
            inner[:, cols] = (gate_part / (1.0 + jnp.exp(-gate_part)) * up_part).astype(
                jnp.bfloat16
            )
            return carry

        lax.fori_loop(0, FFW // 256, hidden, 0)

        def project(n, carry):
            part = jnp.dot(
                inner[...],
                down_w[:, pl.ds(pl.multiple_of(n * 512, 512), 512)],
                preferred_element_type=jnp.float32,
            )
            for j in range(4):
                wide[pl.ds(n * 4 + j, GROUP_ROWS, stride=FEATS), :] = part[
                    :, j * LANES : (j + 1) * LANES
                ]
            return carry

        lax.fori_loop(0, D // 512, project, 0)

        def turn_out(i, carry):
            part = wide[pl.ds(pl.multiple_of(i * 16 * FEATS, 16 * FEATS), 16 * FEATS), :]
            recv[pl.ds(base + i * 16, 16)] = part.reshape(16, FEATS, LANES).astype(jnp.bfloat16)
            return carry

        lax.fori_loop(0, GROUP_ROWS // 16, turn_out, 0)

        def give_back(step, carry):
            pltpu.make_async_remote_copy(
                src_ref=recv.at[chunk(step)],
                dst_ref=back_ref.at[chunk(step)],
                send_sem=out_sem,
                recv_sem=back_sem,
                device_id=source_of(step),
                device_id_type=MESH,
            ).start()
            return carry

        @pl.when(group == 0)
        def _():
            pltpu.make_async_copy(recv.at[chunk(0)], back_ref.at[chunk(0)], back_sem).start()

        lax.fori_loop(
            jnp.maximum(group * GROUP_SLOTS, 1), (group + 1) * GROUP_SLOTS, give_back, 0
        )
        return carry

    lax.fori_loop(0, GROUPS, work, 0)
    far = pl.ds(CAP, ROWS - CAP)
    pltpu.make_async_copy(send.at[far], send.at[far], send_sem).wait()
    pltpu.make_async_copy(recv.at[far], recv.at[far], out_sem).wait()
    pltpu.make_async_copy(back_ref, back_ref, back_sem).wait()


def run_experts(token_of, normed, gate_weight, up_weight, down_weight):
    bf16 = jnp.bfloat16
    anywhere = pl.BlockSpec(memory_space=pl.ANY)
    return pl.pallas_call(
        expert_kernel,
        out_shape=jax.ShapeDtypeStruct((ROWS, FEATS, LANES), bf16),
        in_specs=[
            pl.BlockSpec(memory_space=pltpu.SMEM),
            pl.BlockSpec(memory_space=pltpu.VMEM),
            anywhere,
            anywhere,
            anywhere,
        ],
        out_specs=anywhere,
        scratch_shapes=[
            pltpu.VMEM((D, FFW), bf16),
            pltpu.VMEM((D, FFW), bf16),
            pltpu.VMEM((FFW, D), bf16),
            pltpu.VMEM((ROWS, FEATS, LANES), bf16),
            pltpu.VMEM((ROWS, FEATS, LANES), bf16),
            pltpu.VMEM((GROUP_ROWS, D), bf16),
            pltpu.VMEM((GROUP_ROWS, FFW), bf16),
            pltpu.VMEM((GROUP_ROWS * FEATS, LANES), jnp.float32),
            pltpu.SemaphoreType.DMA((3,)),
            pltpu.SemaphoreType.DMA,
            pltpu.SemaphoreType.DMA((GROUPS,)),
            pltpu.SemaphoreType.DMA,
            pltpu.SemaphoreType.DMA,
        ],
        compiler_params=pltpu.CompilerParams(
            collective_id=0, has_side_effects=True, vmem_limit_bytes=58 * 2**20
        ),
        name="experts",
    )(token_of, normed, gate_weight, up_weight, down_weight)


def combine_kernel(row_ref, gate_ref, back_ref, mixed_ref, cot_ref, out_ref, grad_ref):
    def one(t, carry):
        cot = cot_ref[t].astype(jnp.float32)
        total = mixed_ref[t].astype(jnp.float32)
        sums = []
        for k in range(TOP):
            row = back_ref[row_ref[t * TOP + k]].astype(jnp.float32)
            total = total + gate_ref[t * TOP + k] * row
            sums.append(jnp.sum(cot * row, axis=0, keepdims=True))
        out_ref[t] = total.astype(jnp.bfloat16)
        grad_ref[t] = jnp.concatenate(sums, axis=0)
        return carry

    lax.fori_loop(0, out_ref.shape[0], one, 0)


def combine(row_of, gates, back, mixed, cotangent):
    tok = mixed.shape[0]
    smem = pl.BlockSpec(memory_space=pltpu.SMEM)
    vmem = pl.BlockSpec(memory_space=pltpu.VMEM)
    return pl.pallas_call(
        combine_kernel,
        out_shape=(
            jax.ShapeDtypeStruct((tok, FEATS, LANES), jnp.bfloat16),
            jax.ShapeDtypeStruct((tok, TOP, LANES), jnp.float32),
        ),
        in_specs=[smem, smem, vmem, vmem, vmem],
        out_specs=(vmem, vmem),
        compiler_params=pltpu.CompilerParams(vmem_limit_bytes=40 * 2**20),
        name="combine",
    )(row_of, gates, back, mixed, cotangent)


def routes(ids):
    flat = ids.reshape(-1)
    sp, ep = target_of(jnp.arange(DEVICES, dtype=jnp.int32))
    named = (sp * 16 + ep)[:, None] == jnp.arange(DEVICES, dtype=jnp.int32)[None, :]
    step_of = jnp.sum(named * jnp.arange(DEVICES, dtype=jnp.int32)[:, None], axis=0)
    onehot = (flat[:, None] == jnp.arange(DEVICES, dtype=jnp.int32)[None, :]).astype(jnp.int32)
    place_of = step_of[None, :] * CAP + jnp.cumsum(onehot, axis=0) - 1
    row_of = jnp.sum(place_of * onehot, axis=1)
    token = jnp.arange(flat.shape[0], dtype=jnp.int32) // TOP
    held = row_of[:, None] == jnp.arange(ROWS, dtype=jnp.int32)[None, :]
    token_of = jnp.sum(jnp.where(held, token[:, None], 0), axis=0)
    return row_of.astype(jnp.int32), token_of.astype(jnp.int32)


def body(
    hidden_in,
    queries,
    keys,
    values,
    out_weight,
    norm_gain,
    gate_weight,
    up_weight,
    down_weight,
    expert_ids,
    gates,
    cotangent,
):
    n_seq = lax.axis_size("sp")
    tok = queries.shape[1]
    slab_number = tok * n_seq
    heads_dev = QUERY_HEAD_COUNT // n_seq
    query_group = QUERY_HEAD_COUNT // KEY_VALUE_HEADS
    query_local = queries[0].reshape(tok, n_seq, heads_dev * HEAD_SIZE)
    query_all = lax.all_to_all(query_local, "sp", split_axis=1, concat_axis=0, tiled=True)
    complete_keys, complete_values = (
        lax.all_gather(keys[0], "sp", axis=0, tiled=True),
        lax.all_gather(values[0], "sp", axis=0, tiled=True),
    )
    head_number = lax.axis_index("sp") * heads_dev // query_group
    local_key_rows = lax.dynamic_slice_in_dim(
        complete_keys.reshape(slab_number, KEY_VALUE_HEADS, HEAD_SIZE), head_number, 1, 1
    ).reshape(slab_number, HEAD_SIZE)
    value_mine = lax.dynamic_slice_in_dim(
        complete_values.reshape(slab_number, KEY_VALUE_HEADS, HEAD_SIZE), head_number, 1, 1
    ).reshape(slab_number, HEAD_SIZE)
    query_three = query_all.reshape(slab_number, heads_dev, HEAD_SIZE)
    block = min(512, slab_number)
    scale = 1.0 / np.sqrt(HEAD_SIZE)
    pieces = []
    for block_index in range(slab_number // block):
        first = block_index * block
        finish = first + block
        query_block = query_three[first:finish]
        scores = (
            jnp.einsum(
                "qhd,kd->hqk",
                query_block,
                local_key_rows[:finish],
                preferred_element_type=jnp.float32,
            )
            * scale
        )
        row_pos = first + jnp.arange(block)[:, None]
        col_pos = jnp.arange(finish)[None, :]
        scores = jnp.where((col_pos <= row_pos)[None], scores, jnp.float32(-1e30))
        top = jnp.max(scores, axis=-1, keepdims=True)
        expo = jnp.exp(scores - top)
        probs = (expo / jnp.sum(expo, axis=-1, keepdims=True)).astype(jnp.bfloat16)
        out = jnp.einsum(
            "hqk,kd->qhd", probs, value_mine[:finish], preferred_element_type=jnp.float32
        )
        pieces.append(out.astype(jnp.bfloat16).reshape(block, heads_dev * HEAD_SIZE))
    attended = jnp.concatenate(pieces, axis=0)
    partial_out = jnp.dot(
        attended,
        lax.all_gather(out_weight, "ep", axis=1, tiled=True),
        preferred_element_type=jnp.float32,
    )
    summed = lax.psum_scatter(
        partial_out.astype(jnp.bfloat16), "sp", scatter_dimension=0, tiled=True
    ).astype(jnp.float32)
    mixed_f = (hidden_in[0].astype(jnp.float32) + summed).astype(jnp.bfloat16).astype(jnp.float32)
    inverse = lax.rsqrt(jnp.mean(mixed_f * mixed_f, axis=-1, keepdims=True) + 1e-06)
    normed = (mixed_f * inverse * norm_gain).astype(jnp.bfloat16)
    row_of, token_of = routes(expert_ids[0])
    three = lambda a: a.reshape(tok, FEATS, LANES)
    back = run_experts(token_of, three(normed), gate_weight[0], up_weight[0], down_weight[0])
    out, grads = combine(
        row_of,
        gates[0].reshape(-1),
        back,
        three(mixed_f.astype(jnp.bfloat16)),
        three(cotangent[0]),
    )
    return (out.reshape(1, tok, D), jnp.sum(grads, axis=-1)[None])


def solution(mesh):
    placed = (
        P("ep", "sp", None),
        P("ep", "sp", None),
        P("ep", "sp", None),
        P("ep", "sp", None),
        P("sp", "ep"),
        P(),
        P(("sp", "ep"), None, None),
        P(("sp", "ep"), None, None),
        P(("sp", "ep"), None, None),
        P("ep", "sp", None),
        P("ep", "sp", None),
        P("ep", "sp", None),
    )
    return jax.shard_map(
        body,
        mesh=mesh,
        in_specs=placed,
        out_specs=(P("ep", "sp", None), P("ep", "sp", None)),
        check_vma=False,
    )
```

```python
import jax
import jax.numpy as jnp
import numpy as np
from jax import lax
from jax.experimental import pallas as pl
from jax.experimental.pallas import tpu as pltpu
from jax.sharding import PartitionSpec as P

D = 4096
HEAD_SIZE = 128
TOP = 8


MESH = pl.DeviceIdType.MESH
CAP = 9
DEVICES = 128
ROWS = DEVICES * CAP
GROUPS = 4
GROUP_SLOTS = DEVICES // GROUPS
GROUP_ROWS = GROUP_SLOTS * CAP
FFW = 768
LANES = 128
FEATS = D // LANES


def offset_of(step):
    j = (step * (step + 1) // 2) % DEVICES
    return (j // 16) % 4, j // 64, (j // 4) % 4, j % 4


def place():
    sp, ep = lax.axis_index("sp"), lax.axis_index("ep")
    return sp // 2, sp % 2, ep // 4, ep % 4


def target_of(step):
    z, c, x, y = place()
    dz, dc, dx, dy = offset_of(step)
    turn = 1 - 2 * c
    return (
        ((z + turn * dz + 4) % 4) * 2 + (c + dc) % 2,
        ((x + turn * dx + 4) % 4) * 4 + (y + turn * dy + 4) % 4,
    )


def source_of(step):
    z, c, x, y = place()
    dz, dc, dx, dy = offset_of(step)
    core = (c + dc) % 2
    turn = 1 - 2 * core
    return (
        ((z - turn * dz + 4) % 4) * 2 + core,
        ((x - turn * dx + 4) % 4) * 4 + (y - turn * dy + 4) % 4,
    )


def chunk(step):
    return pl.ds(step * CAP, CAP)


def expert_kernel(
    token_ref,
    normed_ref,
    gate_hbm,
    up_hbm,
    down_hbm,
    back_ref,
    gate_w,
    up_w,
    down_w,
    send,
    recv,
    rows,
    inner,
    wide,
    weight_sem,
    send_sem,
    recv_sem,
    out_sem,
    back_sem,
):
    weights = [
        pltpu.make_async_copy(src, dst, weight_sem.at[i])
        for i, (src, dst) in enumerate(((gate_hbm, gate_w), (up_hbm, up_w), (down_hbm, down_w)))
    ]
    for copy in weights:
        copy.start()

    barrier = pltpu.get_barrier_semaphore()

    def greet(step, carry):
        pl.semaphore_signal(barrier, inc=1, device_id=target_of(step), device_id_type=MESH)
        return carry

    lax.fori_loop(1, DEVICES, greet, 0)

    def fill(step):
        for slot in range(CAP):
            row = step * CAP + slot
            send[row] = normed_ref[token_ref[row]]

    fill(0)
    pl.semaphore_wait(barrier, DEVICES - 1)
    pltpu.make_async_copy(send.at[chunk(0)], recv.at[chunk(0)], recv_sem.at[0]).start()

    def dispatch(step, carry):
        fill(step)
        pltpu.make_async_remote_copy(
            src_ref=send.at[chunk(step)],
            dst_ref=recv.at[chunk(step)],
            send_sem=send_sem,
            recv_sem=recv_sem.at[step // GROUP_SLOTS],
            device_id=target_of(step),
            device_id_type=MESH,
        ).start()
        return carry

    lax.fori_loop(1, DEVICES, dispatch, 0)
    for copy in weights:
        copy.wait()

    def work(group, carry):
        base = group * GROUP_ROWS
        block = pl.ds(base, GROUP_ROWS)
        pltpu.make_async_copy(recv.at[block], recv.at[block], recv_sem.at[group]).wait()

        def turn_in(i, carry):
            wide[pl.ds(0, 16 * FEATS), :] = (
                recv[pl.ds(base + i * 16, 16)].astype(jnp.float32).reshape(16 * FEATS, LANES)
            )
            for f in range(FEATS):
                rows[pl.ds(pl.multiple_of(i * 16, 16), 16), f * LANES : (f + 1) * LANES] = wide[
                    pl.ds(f, 16, stride=FEATS), :
                ].astype(jnp.bfloat16)
            return carry

        lax.fori_loop(0, GROUP_ROWS // 16, turn_in, 0)

        def hidden(n, carry):
            cols = pl.ds(pl.multiple_of(n * 256, 256), 256)
            gate_part = jnp.dot(rows[...], gate_w[:, cols], preferred_element_type=jnp.float32)
            up_part = jnp.dot(rows[...], up_w[:, cols], preferred_element_type=jnp.float32)
            inner[:, cols] = (gate_part / (1.0 + jnp.exp(-gate_part)) * up_part).astype(
                jnp.bfloat16
            )
            return carry

        lax.fori_loop(0, FFW // 256, hidden, 0)

        def project(n, carry):
            part = jnp.dot(
                inner[...],
                down_w[:, pl.ds(pl.multiple_of(n * 512, 512), 512)],
                preferred_element_type=jnp.float32,
            )
            for j in range(4):
                wide[pl.ds(n * 4 + j, GROUP_ROWS, stride=FEATS), :] = part[
                    :, j * LANES : (j + 1) * LANES
                ]
            return carry

        lax.fori_loop(0, D // 512, project, 0)

        def turn_out(i, carry):
            part = wide[pl.ds(pl.multiple_of(i * 16 * FEATS, 16 * FEATS), 16 * FEATS), :]
            recv[pl.ds(base + i * 16, 16)] = part.reshape(16, FEATS, LANES).astype(jnp.bfloat16)
            return carry

        lax.fori_loop(0, GROUP_ROWS // 16, turn_out, 0)

        def give_back(step, carry):
            pltpu.make_async_remote_copy(
                src_ref=recv.at[chunk(step)],
                dst_ref=back_ref.at[chunk(step)],
                send_sem=out_sem,
                recv_sem=back_sem,
                device_id=source_of(step),
                device_id_type=MESH,
            ).start()
            return carry

        @pl.when(group == 0)
        def _():
            pltpu.make_async_copy(recv.at[chunk(0)], back_ref.at[chunk(0)], back_sem).start()

        lax.fori_loop(
            jnp.maximum(group * GROUP_SLOTS, 1), (group + 1) * GROUP_SLOTS, give_back, 0
        )
        return carry

    lax.fori_loop(0, GROUPS, work, 0)
    far = pl.ds(CAP, ROWS - CAP)
    pltpu.make_async_copy(send.at[far], send.at[far], send_sem).wait()
    pltpu.make_async_copy(recv.at[far], recv.at[far], out_sem).wait()
    pltpu.make_async_copy(back_ref, back_ref, back_sem).wait()


def run_experts(token_of, normed, gate_weight, up_weight, down_weight):
    bf16 = jnp.bfloat16
    anywhere = pl.BlockSpec(memory_space=pl.ANY)
    return pl.pallas_call(
        expert_kernel,
        out_shape=jax.ShapeDtypeStruct((ROWS, FEATS, LANES), bf16),
        in_specs=[
            pl.BlockSpec(memory_space=pltpu.SMEM),
            pl.BlockSpec(memory_space=pltpu.VMEM),
            anywhere,
            anywhere,
            anywhere,
        ],
        out_specs=anywhere,
        scratch_shapes=[
            pltpu.VMEM((D, FFW), bf16),
            pltpu.VMEM((D, FFW), bf16),
            pltpu.VMEM((FFW, D), bf16),
            pltpu.VMEM((ROWS, FEATS, LANES), bf16),
            pltpu.VMEM((ROWS, FEATS, LANES), bf16),
            pltpu.VMEM((GROUP_ROWS, D), bf16),
            pltpu.VMEM((GROUP_ROWS, FFW), bf16),
            pltpu.VMEM((GROUP_ROWS * FEATS, LANES), jnp.float32),
            pltpu.SemaphoreType.DMA((3,)),
            pltpu.SemaphoreType.DMA,
            pltpu.SemaphoreType.DMA((GROUPS,)),
            pltpu.SemaphoreType.DMA,
            pltpu.SemaphoreType.DMA,
        ],
        compiler_params=pltpu.CompilerParams(
            collective_id=0, has_side_effects=True, vmem_limit_bytes=58 * 2**20
        ),
        name="experts",
    )(token_of, normed, gate_weight, up_weight, down_weight)


def combine_kernel(row_ref, gate_ref, back_ref, mixed_ref, cot_ref, out_ref, grad_ref):
    def one(t, carry):
        cot = cot_ref[t].astype(jnp.float32)
        total = mixed_ref[t].astype(jnp.float32)
        sums = []
        for k in range(TOP):
            row = back_ref[row_ref[t * TOP + k]].astype(jnp.float32)
            total = total + gate_ref[t * TOP + k] * row
            sums.append(jnp.sum(cot * row, axis=0, keepdims=True))
        out_ref[t] = total.astype(jnp.bfloat16)
        grad_ref[t] = jnp.concatenate(sums, axis=0)
        return carry

    lax.fori_loop(0, out_ref.shape[0], one, 0)


def combine(row_of, gates, back, mixed, cotangent):
    tok = mixed.shape[0]
    smem = pl.BlockSpec(memory_space=pltpu.SMEM)
    vmem = pl.BlockSpec(memory_space=pltpu.VMEM)
    return pl.pallas_call(
        combine_kernel,
        out_shape=(
            jax.ShapeDtypeStruct((tok, FEATS, LANES), jnp.bfloat16),
            jax.ShapeDtypeStruct((tok, TOP, LANES), jnp.float32),
        ),
        in_specs=[smem, smem, vmem, vmem, vmem],
        out_specs=(vmem, vmem),
        compiler_params=pltpu.CompilerParams(vmem_limit_bytes=40 * 2**20),
        name="combine",
    )(row_of, gates, back, mixed, cotangent)


def routes(ids):
    flat = ids.reshape(-1)
    sp, ep = target_of(jnp.arange(DEVICES, dtype=jnp.int32))
    named = (sp * 16 + ep)[:, None] == jnp.arange(DEVICES, dtype=jnp.int32)[None, :]
    step_of = jnp.sum(named * jnp.arange(DEVICES, dtype=jnp.int32)[:, None], axis=0)
    onehot = (flat[:, None] == jnp.arange(DEVICES, dtype=jnp.int32)[None, :]).astype(jnp.int32)
    place_of = step_of[None, :] * CAP + jnp.cumsum(onehot, axis=0) - 1
    row_of = jnp.sum(place_of * onehot, axis=1)
    token = jnp.arange(flat.shape[0], dtype=jnp.int32) // TOP
    held = row_of[:, None] == jnp.arange(ROWS, dtype=jnp.int32)[None, :]
    token_of = jnp.sum(jnp.where(held, token[:, None], 0), axis=0)
    return row_of.astype(jnp.int32), token_of.astype(jnp.int32)


HEAD_BLOCK = 8 * HEAD_SIZE
TOK = 128
ZS = 4
WIDE = 256
BLOCKS = D // WIDE
HALF = 256


def mix_kernel(
    query_ref,
    key_ref,
    value_ref,
    weight_ref,
    hidden_ref,
    gain_ref,
    mixed_ref,
    normed_ref,
    q_all,
    k_all,
    v_all,
    w_all,
    att,
    part,
    relay,
    final,
    q_send,
    q_recv,
    k_send,
    k_recv,
    v_send,
    v_recv,
    w1_send,
    w1_recv,
    w2_send,
    w2_recv,
    wd_send,
    wd_recv,
    rs_send,
    relay_recv,
    final_recv,
):
    z, c, x, y = place()
    sp, ep = z * 2 + c, x * 4 + y

    def remote(src, dst, send_sem, recv_sem, to):
        pltpu.make_async_remote_copy(
            src_ref=src,
            dst_ref=dst,
            send_sem=send_sem,
            recv_sem=recv_sem,
            device_id=to,
            device_id_type=MESH,
        ).start()

    def local(src, dst, sem):
        pltpu.make_async_copy(src, dst, sem).start()

    def settle(ref, sem):
        pltpu.make_async_copy(ref, ref, sem).wait()

    barrier = pltpu.get_barrier_semaphore()
    for d in range(1, 8):
        pl.semaphore_signal(barrier, inc=1, device_id=((sp + d) % 8, ep), device_id_type=MESH)
    for d in range(1, 4):
        along_x, along_y = (sp, ((x + d) % 4) * 4 + y), (sp, x * 4 + (y + d) % 4)
        pl.semaphore_signal(barrier, inc=1, device_id=along_x, device_id_type=MESH)
        pl.semaphore_signal(barrier, inc=1, device_id=along_y, device_id_type=MESH)
    pl.semaphore_wait(barrier, 13)

    def group_of(other):
        return pl.ds(pl.multiple_of(other // 4 * HEAD_SIZE, HEAD_SIZE), HEAD_SIZE)

    def heads_of(chip):
        return pl.ds(pl.multiple_of(chip * HEAD_BLOCK, HEAD_BLOCK), HEAD_BLOCK)

    top, low = pl.ds(0, HALF), pl.ds(HALF, HALF)
    for d in range(1, 8):
        other = (sp + d) % 8
        remote(key_ref.at[:, group_of(other)], k_all.at[sp], k_send, k_recv, (other, ep))
        remote(value_ref.at[:, group_of(other)], v_all.at[sp], v_send, v_recv, (other, ep))
    for d in range(1, 4):
        along_x, along_y = (sp, ((x + d) % 4) * 4 + y), (sp, x * 4 + (y + d) % 4)
        remote(weight_ref.at[top], w_all.at[ep, c, top], w1_send.at[0], w1_recv.at[0], along_x)
        remote(weight_ref.at[low], w_all.at[ep, c, low], w1_send.at[1], w1_recv.at[1], along_y)
    for d in (1, 3, 2):
        chip = (z + d) % 4
        remote(
            query_ref.at[:, heads_of(chip)], q_all.at[z], q_send, q_recv.at[z], (chip * 2 + c, ep)
        )
    local(key_ref.at[:, group_of(sp)], k_all.at[sp], k_recv)
    local(value_ref.at[:, group_of(sp)], v_all.at[sp], v_recv)
    local(query_ref.at[:, heads_of(z)], q_all.at[z], q_recv.at[z])
    local(weight_ref.at[top], w_all.at[ep, c, top], w1_recv.at[0])
    local(weight_ref.at[low], w_all.at[ep, c, low], w1_recv.at[1])

    settle(w_all.at[pl.ds(0, 2), 0], w1_recv.at[0])
    settle(w_all.at[pl.ds(0, 2), 0], w1_recv.at[1])
    twin = (z * 2 + 1 - c, ep)

    def second(i, carry):
        d, k = i // 4 + 1, i % 4
        mine = w_all.at[k * 4 + y, c, top]
        remote(mine, mine, w2_send.at[0], w2_recv.at[0], (sp, x * 4 + (y + d) % 4))
        mine = w_all.at[x * 4 + k, c, low]
        remote(mine, mine, w2_send.at[1], w2_recv.at[1], (sp, ((x + d) % 4) * 4 + y))
        return carry

    lax.fori_loop(0, 12, second, 0)

    def share_first(k, carry):
        mine = w_all.at[k * 4 + y, c, top]
        remote(mine, mine, wd_send, wd_recv, twin)
        mine = w_all.at[x * 4 + k, c, low]
        remote(mine, mine, wd_send, wd_recv, twin)
        return carry

    lax.fori_loop(0, 4, share_first, 0)

    settle(k_all, k_recv)
    settle(v_all, v_recv)
    scale = np.float32(1.0 / np.sqrt(HEAD_SIZE))

    def attend(block):
        settle(q_all.at[block], q_recv.at[block])
        count = 2 * block + 2
        length = count * TOK

        def heads(pair, carry):
            cols = pl.ds(pl.multiple_of(pair * 256, 256), 256)
            both = q_all[block, :, cols]
            rows = jnp.concatenate([both[:, :HEAD_SIZE], both[:, HEAD_SIZE:]], axis=0)
            scores = (
                lax.dot_general(
                    rows,
                    k_all[0:count].reshape(length, HEAD_SIZE),
                    (((1,), (1,)), ((), ())),
                    preferred_element_type=jnp.float32,
                )
                * scale
            )
            row = lax.broadcasted_iota(jnp.int32, (2 * TOK, length), 0) % TOK + (
                2 * block + c
            ) * TOK
            col = lax.broadcasted_iota(jnp.int32, (2 * TOK, length), 1)
            scores = jnp.where(col <= row, scores, jnp.float32(-1e30))
            expo = jnp.exp(scores - jnp.max(scores, axis=-1, keepdims=True))
            probs = (expo / jnp.sum(expo, axis=-1, keepdims=True)).astype(jnp.bfloat16)
            out = jnp.dot(
                probs, v_all[0:count].reshape(length, HEAD_SIZE), preferred_element_type=jnp.float32
            ).astype(jnp.bfloat16)
            att[block * TOK : (block + 1) * TOK, cols] = jnp.concatenate(
                [out[:TOK], out[TOK:]], axis=1
            )
            return carry

        lax.fori_loop(0, 4, heads, 0)

    attend(0)
    attend(1)
    attend(2)
    settle(w_all.at[pl.ds(0, 6), 0], w2_recv.at[0])
    settle(w_all.at[pl.ds(0, 6), 0], w2_recv.at[1])

    def share_second(i, carry):
        d, k = i // 4 + 1, i % 4
        mine = w_all.at[k * 4 + (y + d) % 4, c, top]
        remote(mine, mine, wd_send, wd_recv, twin)
        mine = w_all.at[((x + d) % 4) * 4 + k, c, low]
        remote(mine, mine, wd_send, wd_recv, twin)
        return carry

    lax.fori_loop(0, 12, share_second, 0)
    attend(3)
    settle(w_all.at[pl.ds(0, 16), 0], wd_recv)

    after, before, across = (z + 1) % 4, (z + 3) % 4, (z + 2) % 4
    sides = ((after * 2 + c, ep), (before * 2 + c, ep))

    def project(pair, carry):
        for odd in range(2):
            j = pair * 2 + odd
            part[j] = (
                jnp.dot(
                    att[...], w_all[j].reshape(2 * 512, WIDE), preferred_element_type=jnp.float32
                )
                .astype(jnp.bfloat16)
                .reshape(ZS, TOK, WIDE)
            )
            relay_to, straight_to = sides[odd], sides[1 - odd]
            straight = (before, after)[odd]
            remote(part.at[j, across], relay.at[j], rs_send, relay_recv.at[j], relay_to)
            remote(
                part.at[j, straight],
                final.at[1 - odd, j],
                rs_send,
                final_recv.at[1 - odd, j],
                straight_to,
            )
        return carry

    lax.fori_loop(0, BLOCKS // 2, project, 0)

    def pass_on(pair, carry):
        for odd in range(2):
            j = pair * 2 + odd
            onward = (after, before)[odd]
            settle(relay.at[j], relay_recv.at[j])
            part[j, onward] = (
                part[j, onward].astype(jnp.float32) + relay[j].astype(jnp.float32)
            ).astype(jnp.bfloat16)
            remote(
                part.at[j, onward], final.at[odd, j], rs_send, final_recv.at[odd, j], sides[odd]
            )
        return carry

    lax.fori_loop(0, BLOCKS // 2, pass_on, 0)

    def finish(j, squares):
        for side in range(2):
            settle(final.at[side, j], final_recv.at[side, j])
        cols = pl.ds(pl.multiple_of(j * WIDE, WIDE), WIDE)
        total = hidden_ref[:, cols].astype(jnp.float32) + part[j, z].astype(jnp.float32)
        total = total + final[0, j].astype(jnp.float32) + final[1, j].astype(jnp.float32)
        mixed = total.astype(jnp.bfloat16)
        mixed_ref[:, cols] = mixed
        wide = mixed.astype(jnp.float32)
        wide = wide * wide
        return squares + wide[:, :LANES] + wide[:, LANES:]

    squares = lax.fori_loop(0, BLOCKS, finish, jnp.zeros((TOK, LANES), jnp.float32))
    inverse = lax.rsqrt(jnp.sum(squares, axis=-1, keepdims=True) * np.float32(1.0 / D) + 1e-06)

    def norm(j, carry):
        cols = pl.ds(pl.multiple_of(j * WIDE, WIDE), WIDE)
        normed_ref[:, cols] = (
            mixed_ref[:, cols].astype(jnp.float32) * inverse * gain_ref[:, cols]
        ).astype(jnp.bfloat16)
        return carry

    lax.fori_loop(0, BLOCKS, norm, 0)

    settle(q_all.at[pl.ds(0, 3)], q_send)
    settle(k_all.at[pl.ds(0, 7)], k_send)
    settle(v_all.at[pl.ds(0, 7)], v_send)
    for i in range(2):
        settle(w_all.at[pl.ds(0, 3), 0, top], w1_send.at[i])
        settle(w_all.at[pl.ds(0, 6), 0], w2_send.at[i])
    settle(w_all.at[pl.ds(0, 16), 0], wd_send)
    settle(part.at[:, pl.ds(0, 3)], rs_send)


def mix(queries, keys, values, out_weight, hidden, gain):
    bf16 = jnp.bfloat16
    vmem = pl.BlockSpec(memory_space=pltpu.VMEM)
    dma = pltpu.SemaphoreType.DMA
    shape = jax.ShapeDtypeStruct((TOK, D), bf16)
    return pl.pallas_call(
        mix_kernel,
        out_shape=(shape, shape),
        in_specs=[vmem] * 6,
        out_specs=(vmem, vmem),
        scratch_shapes=[
            pltpu.VMEM((ZS, TOK, HEAD_BLOCK), bf16),
            pltpu.VMEM((8, TOK, HEAD_SIZE), bf16),
            pltpu.VMEM((8, TOK, HEAD_SIZE), bf16),
            pltpu.VMEM((BLOCKS, 2, 512, WIDE), bf16),
            pltpu.VMEM((ZS * TOK, HEAD_BLOCK), bf16),
            pltpu.VMEM((BLOCKS, ZS, TOK, WIDE), bf16),
            pltpu.VMEM((BLOCKS, TOK, WIDE), bf16),
            pltpu.VMEM((2, BLOCKS, TOK, WIDE), bf16),
            dma,
            dma((ZS,)),
            dma,
            dma,
            dma,
            dma,
            dma((2,)),
            dma((2,)),
            dma((2,)),
            dma((2,)),
            dma,
            dma,
            dma,
            dma((BLOCKS,)),
            dma((2, BLOCKS)),
        ],
        compiler_params=pltpu.CompilerParams(
            collective_id=1, has_side_effects=True, vmem_limit_bytes=48 * 2**20
        ),
        name="mix",
    )(queries, keys, values, out_weight, hidden, gain)


def body(
    hidden_in,
    queries,
    keys,
    values,
    out_weight,
    norm_gain,
    gate_weight,
    up_weight,
    down_weight,
    expert_ids,
    gates,
    cotangent,
):
    tok = queries.shape[1]
    mixed, normed = mix(
        queries[0], keys[0], values[0], out_weight, hidden_in[0], norm_gain.reshape(1, D)
    )
    row_of, token_of = routes(expert_ids[0])
    three = lambda a: a.reshape(tok, FEATS, LANES)
    back = run_experts(token_of, three(normed), gate_weight[0], up_weight[0], down_weight[0])
    out, grads = combine(
        row_of,
        gates[0].reshape(-1),
        back,
        three(mixed),
        three(cotangent[0]),
    )
    return (out.reshape(1, tok, D), jnp.sum(grads, axis=-1)[None])


def solution(mesh):
    placed = (
        P("ep", "sp", None),
        P("ep", "sp", None),
        P("ep", "sp", None),
        P("ep", "sp", None),
        P("sp", "ep"),
        P(),
        P(("sp", "ep"), None, None),
        P(("sp", "ep"), None, None),
        P(("sp", "ep"), None, None),
        P("ep", "sp", None),
        P("ep", "sp", None),
        P("ep", "sp", None),
    )
    return jax.shard_map(
        body,
        mesh=mesh,
        in_specs=placed,
        out_specs=(P("ep", "sp", None), P("ep", "sp", None)),
        check_vma=False,
    )
```

```python
import jax
import jax.numpy as jnp
import numpy as np
from jax import lax
from jax.experimental import pallas as pl
from jax.experimental.pallas import tpu as pltpu
from jax.sharding import PartitionSpec as P

D = 4096
HEAD_SIZE = 128
TOP = 8


MESH = pl.DeviceIdType.MESH
CAP = 9
DEVICES = 128
ROWS = DEVICES * CAP
GROUPS = 8
GROUP_SLOTS = DEVICES // GROUPS
GROUP_ROWS = GROUP_SLOTS * CAP
FFW = 768
LANES = 128
FEATS = D // LANES


def offset_of(step):
    j = (step * (step + 1) // 2) % DEVICES
    return (j // 16) % 4, j // 64, (j // 4) % 4, j % 4


def place():
    sp, ep = lax.axis_index("sp"), lax.axis_index("ep")
    return sp // 2, sp % 2, ep // 4, ep % 4


def target_of(step):
    z, c, x, y = place()
    dz, dc, dx, dy = offset_of(step)
    turn = 1 - 2 * c
    return (
        ((z + turn * dz + 4) % 4) * 2 + (c + dc) % 2,
        ((x + turn * dx + 4) % 4) * 4 + (y + turn * dy + 4) % 4,
    )


def source_of(step):
    z, c, x, y = place()
    dz, dc, dx, dy = offset_of(step)
    core = (c + dc) % 2
    turn = 1 - 2 * core
    return (
        ((z - turn * dz + 4) % 4) * 2 + core,
        ((x - turn * dx + 4) % 4) * 4 + (y - turn * dy + 4) % 4,
    )


def chunk(step):
    return pl.ds(step * CAP, CAP)


def expert_kernel(
    token_ref,
    row_ref,
    scale_ref,
    normed_ref,
    mixed_ref,
    cot_ref,
    gate_hbm,
    up_hbm,
    down_hbm,
    out_ref,
    grad_ref,
    back_ref,
    gate_w,
    up_w,
    down_w,
    send,
    recv,
    rows,
    inner,
    wide,
    weight_sem,
    send_sem,
    recv_sem,
    out_sem,
    back_sem,
):
    weights = [
        pltpu.make_async_copy(src, dst, weight_sem.at[i])
        for i, (src, dst) in enumerate(((gate_hbm, gate_w), (up_hbm, up_w), (down_hbm, down_w)))
    ]
    for copy in weights:
        copy.start()

    barrier = pltpu.get_barrier_semaphore()

    def greet(step, carry):
        pl.semaphore_signal(barrier, inc=1, device_id=target_of(step), device_id_type=MESH)
        return carry

    lax.fori_loop(1, DEVICES, greet, 0)

    def fill(step):
        for slot in range(CAP):
            row = step * CAP + slot
            send[row] = normed_ref[token_ref[row]]

    fill(0)
    pl.semaphore_wait(barrier, DEVICES - 1)
    pltpu.make_async_copy(send.at[chunk(0)], recv.at[chunk(0)], recv_sem.at[0]).start()

    def dispatch(step, carry):
        fill(step)
        pltpu.make_async_remote_copy(
            src_ref=send.at[chunk(step)],
            dst_ref=recv.at[chunk(step)],
            send_sem=send_sem,
            recv_sem=recv_sem.at[step // GROUP_SLOTS],
            device_id=target_of(step),
            device_id_type=MESH,
        ).start()
        return carry

    lax.fori_loop(1, DEVICES, dispatch, 0)
    for copy in weights:
        copy.wait()

    def work(group, carry):
        base = group * GROUP_ROWS
        block = pl.ds(base, GROUP_ROWS)
        pltpu.make_async_copy(recv.at[block], recv.at[block], recv_sem.at[group]).wait()

        def turn_in(i, carry):
            wide[pl.ds(0, 16 * FEATS), :] = (
                recv[pl.ds(base + i * 16, 16)].astype(jnp.float32).reshape(16 * FEATS, LANES)
            )
            for f in range(FEATS):
                rows[pl.ds(pl.multiple_of(i * 16, 16), 16), f * LANES : (f + 1) * LANES] = wide[
                    pl.ds(f, 16, stride=FEATS), :
                ].astype(jnp.bfloat16)
            return carry

        lax.fori_loop(0, GROUP_ROWS // 16, turn_in, 0)

        def hidden(n, carry):
            cols = pl.ds(pl.multiple_of(n * 256, 256), 256)
            gate_part = jnp.dot(rows[...], gate_w[:, cols], preferred_element_type=jnp.float32)
            up_part = jnp.dot(rows[...], up_w[:, cols], preferred_element_type=jnp.float32)
            inner[:, cols] = (gate_part / (1.0 + jnp.exp(-gate_part)) * up_part).astype(
                jnp.bfloat16
            )
            return carry

        lax.fori_loop(0, FFW // 256, hidden, 0)

        def project(n, carry):
            part = jnp.dot(
                inner[...],
                down_w[:, pl.ds(pl.multiple_of(n * 512, 512), 512)],
                preferred_element_type=jnp.float32,
            )
            for j in range(4):
                wide[pl.ds(n * 4 + j, GROUP_ROWS, stride=FEATS), :] = part[
                    :, j * LANES : (j + 1) * LANES
                ]
            return carry

        lax.fori_loop(0, D // 512, project, 0)

        def turn_out(i, carry):
            part = wide[pl.ds(pl.multiple_of(i * 16 * FEATS, 16 * FEATS), 16 * FEATS), :]
            recv[pl.ds(base + i * 16, 16)] = part.reshape(16, FEATS, LANES).astype(jnp.bfloat16)
            return carry

        lax.fori_loop(0, GROUP_ROWS // 16, turn_out, 0)

        def give_back(step, carry):
            pltpu.make_async_remote_copy(
                src_ref=recv.at[chunk(step)],
                dst_ref=back_ref.at[chunk(step)],
                send_sem=out_sem,
                recv_sem=back_sem,
                device_id=source_of(step),
                device_id_type=MESH,
            ).start()
            return carry

        @pl.when(group == 0)
        def _():
            pltpu.make_async_copy(recv.at[chunk(0)], back_ref.at[chunk(0)], back_sem).start()

        lax.fori_loop(
            jnp.maximum(group * GROUP_SLOTS, 1), (group + 1) * GROUP_SLOTS, give_back, 0
        )
        return carry

    lax.fori_loop(0, GROUPS, work, 0)
    far = pl.ds(CAP, ROWS - CAP)
    pltpu.make_async_copy(send.at[far], send.at[far], send_sem).wait()
    pltpu.make_async_copy(recv.at[far], recv.at[far], out_sem).wait()
    pltpu.make_async_copy(back_ref, back_ref, back_sem).wait()

    def combine(t, carry):
        cot = cot_ref[t].astype(jnp.float32)
        total = mixed_ref[t].astype(jnp.float32)
        sums = []
        for k in range(TOP):
            row = back_ref[row_ref[t * TOP + k]].astype(jnp.float32)
            total = total + scale_ref[t * TOP + k] * row
            sums.append(jnp.sum(cot * row, axis=0, keepdims=True))
        wide[pl.ds(pl.multiple_of(t * FEATS, FEATS), FEATS), :] = total
        grad_ref[t] = jnp.concatenate(sums, axis=0)
        return carry

    lax.fori_loop(0, out_ref.shape[0], combine, 0)

    def lay_out(i, carry):
        for f in range(FEATS):
            out_ref[pl.ds(pl.multiple_of(i * 16, 16), 16), f * LANES : (f + 1) * LANES] = wide[
                pl.ds(i * 16 * FEATS + f, 16, stride=FEATS), :
            ].astype(jnp.bfloat16)
        return carry

    lax.fori_loop(0, out_ref.shape[0] // 16, lay_out, 0)


def run_experts(
    token_of, row_of, gates, normed, mixed, cotangent, gate_weight, up_weight, down_weight
):
    bf16 = jnp.bfloat16
    tok = normed.shape[0]
    anywhere = pl.BlockSpec(memory_space=pl.ANY)
    smem = pl.BlockSpec(memory_space=pltpu.SMEM)
    vmem = pl.BlockSpec(memory_space=pltpu.VMEM)
    return pl.pallas_call(
        expert_kernel,
        out_shape=(
            jax.ShapeDtypeStruct((tok, D), bf16),
            jax.ShapeDtypeStruct((tok, TOP, LANES), jnp.float32),
        ),
        in_specs=[smem, smem, smem, vmem, vmem, vmem, anywhere, anywhere, anywhere],
        out_specs=(vmem, vmem),
        scratch_shapes=[
            pltpu.VMEM((ROWS, FEATS, LANES), bf16),
            pltpu.VMEM((D, FFW), bf16),
            pltpu.VMEM((D, FFW), bf16),
            pltpu.VMEM((FFW, D), bf16),
            pltpu.VMEM((ROWS, FEATS, LANES), bf16),
            pltpu.VMEM((ROWS, FEATS, LANES), bf16),
            pltpu.VMEM((GROUP_ROWS, D), bf16),
            pltpu.VMEM((GROUP_ROWS, FFW), bf16),
            pltpu.VMEM((GROUP_ROWS * FEATS, LANES), jnp.float32),
            pltpu.SemaphoreType.DMA((3,)),
            pltpu.SemaphoreType.DMA,
            pltpu.SemaphoreType.DMA((GROUPS,)),
            pltpu.SemaphoreType.DMA,
            pltpu.SemaphoreType.DMA,
        ],
        compiler_params=pltpu.CompilerParams(
            collective_id=0, has_side_effects=True, vmem_limit_bytes=58 * 2**20
        ),
        name="experts",
    )(token_of, row_of, gates, normed, mixed, cotangent, gate_weight, up_weight, down_weight)


def routes(ids):
    flat = ids.reshape(-1)
    sp, ep = target_of(jnp.arange(DEVICES, dtype=jnp.int32))
    named = (sp * 16 + ep)[:, None] == jnp.arange(DEVICES, dtype=jnp.int32)[None, :]
    step_of = jnp.sum(named * jnp.arange(DEVICES, dtype=jnp.int32)[:, None], axis=0)
    onehot = (flat[:, None] == jnp.arange(DEVICES, dtype=jnp.int32)[None, :]).astype(jnp.int32)
    place_of = step_of[None, :] * CAP + jnp.cumsum(onehot, axis=0) - 1
    row_of = jnp.sum(place_of * onehot, axis=1)
    token = jnp.arange(flat.shape[0], dtype=jnp.int32) // TOP
    held = row_of[:, None] == jnp.arange(ROWS, dtype=jnp.int32)[None, :]
    token_of = jnp.sum(jnp.where(held, token[:, None], 0), axis=0)
    return row_of.astype(jnp.int32), token_of.astype(jnp.int32)


HEAD_BLOCK = 8 * HEAD_SIZE
TOK = 128
ZS = 4
WIDE = 256
BLOCKS = D // WIDE
HALF = 256


def mix_kernel(
    query_ref,
    key_ref,
    value_ref,
    weight_ref,
    hidden_ref,
    gain_ref,
    mixed_ref,
    normed_ref,
    q_all,
    k_all,
    v_all,
    w_all,
    att,
    part,
    relay,
    final,
    held,
    q_send,
    q_recv,
    k_send,
    k_recv,
    v_send,
    v_recv,
    w1_send,
    w1_recv,
    w2_send,
    w2_recv,
    wd_send,
    wd_recv,
    rs_send,
    relay_recv,
    final_recv,
    held_sem,
):
    z, c, x, y = place()
    sp, ep = z * 2 + c, x * 4 + y

    def remote(src, dst, send_sem, recv_sem, to):
        pltpu.make_async_remote_copy(
            src_ref=src,
            dst_ref=dst,
            send_sem=send_sem,
            recv_sem=recv_sem,
            device_id=to,
            device_id_type=MESH,
        ).start()

    def local(src, dst, sem):
        pltpu.make_async_copy(src, dst, sem).start()

    def settle(ref, sem):
        pltpu.make_async_copy(ref, ref, sem).wait()

    local(hidden_ref, held, held_sem)
    barrier = pltpu.get_barrier_semaphore()
    for d in range(1, 8):
        pl.semaphore_signal(barrier, inc=1, device_id=((sp + d) % 8, ep), device_id_type=MESH)
    for d in range(1, 4):
        along_x, along_y = (sp, ((x + d) % 4) * 4 + y), (sp, x * 4 + (y + d) % 4)
        pl.semaphore_signal(barrier, inc=1, device_id=along_x, device_id_type=MESH)
        pl.semaphore_signal(barrier, inc=1, device_id=along_y, device_id_type=MESH)
    pl.semaphore_wait(barrier, 13)

    def group_of(other):
        return pl.ds(pl.multiple_of(other // 4 * HEAD_SIZE, HEAD_SIZE), HEAD_SIZE)

    def heads_of(chip):
        return pl.ds(pl.multiple_of(chip * HEAD_BLOCK, HEAD_BLOCK), HEAD_BLOCK)

    top, low = pl.ds(0, HALF), pl.ds(HALF, HALF)
    for d in range(1, 8):
        other = (sp + d) % 8
        remote(key_ref.at[:, group_of(other)], k_all.at[sp], k_send, k_recv, (other, ep))
        remote(value_ref.at[:, group_of(other)], v_all.at[sp], v_send, v_recv, (other, ep))
    for d in range(1, 4):
        along_x, along_y = (sp, ((x + d) % 4) * 4 + y), (sp, x * 4 + (y + d) % 4)
        remote(weight_ref.at[top], w_all.at[ep, c, top], w1_send.at[0], w1_recv.at[0], along_x)
        remote(weight_ref.at[low], w_all.at[ep, c, low], w1_send.at[1], w1_recv.at[1], along_y)
    for d in (1, 3, 2):
        chip = (z + d) % 4
        remote(
            query_ref.at[:, heads_of(chip)], q_all.at[z], q_send, q_recv.at[z], (chip * 2 + c, ep)
        )
    local(key_ref.at[:, group_of(sp)], k_all.at[sp], k_recv)
    local(value_ref.at[:, group_of(sp)], v_all.at[sp], v_recv)
    local(query_ref.at[:, heads_of(z)], q_all.at[z], q_recv.at[z])
    local(weight_ref.at[top], w_all.at[ep, c, top], w1_recv.at[0])
    local(weight_ref.at[low], w_all.at[ep, c, low], w1_recv.at[1])

    settle(w_all.at[pl.ds(0, 2), 0], w1_recv.at[0])
    settle(w_all.at[pl.ds(0, 2), 0], w1_recv.at[1])
    twin = (z * 2 + 1 - c, ep)

    def second(d):
        def send(k, carry):
            mine = w_all.at[k * 4 + y, c, top]
            remote(mine, mine, w2_send.at[0], w2_recv.at[0, d], (sp, x * 4 + (y + d) % 4))
            mine = w_all.at[x * 4 + k, c, low]
            remote(mine, mine, w2_send.at[1], w2_recv.at[1, d], (sp, ((x + d) % 4) * 4 + y))
            return carry

        lax.fori_loop(0, 4, send, 0)

    for d in (1, 3, 2):
        second(d)

    def share(d):
        def send(k, carry):
            mine = w_all.at[k * 4 + (y + 4 - d) % 4, c, top]
            remote(mine, mine, wd_send, wd_recv.at[d], twin)
            mine = w_all.at[((x + 4 - d) % 4) * 4 + k, c, low]
            remote(mine, mine, wd_send, wd_recv.at[d], twin)
            return carry

        lax.fori_loop(0, 4, send, 0)

    def arrive(d):
        settle(w_all.at[pl.ds(0, 2), 0], w2_recv.at[0, d])
        settle(w_all.at[pl.ds(0, 2), 0], w2_recv.at[1, d])
        share(d)

    share(0)

    settle(k_all, k_recv)
    settle(v_all, v_recv)
    scale = np.float32(1.0 / np.sqrt(HEAD_SIZE))

    def attend(block):
        settle(q_all.at[block], q_recv.at[block])
        count = 2 * block + 2
        length = count * TOK

        def heads(pair, carry):
            cols = pl.ds(pl.multiple_of(pair * 256, 256), 256)
            both = q_all[block, :, cols]
            rows = jnp.concatenate([both[:, :HEAD_SIZE], both[:, HEAD_SIZE:]], axis=0)
            scores = (
                lax.dot_general(
                    rows,
                    k_all[0:count].reshape(length, HEAD_SIZE),
                    (((1,), (1,)), ((), ())),
                    preferred_element_type=jnp.float32,
                )
                * scale
            )
            row = lax.broadcasted_iota(jnp.int32, (2 * TOK, length), 0) % TOK + (
                2 * block + c
            ) * TOK
            col = lax.broadcasted_iota(jnp.int32, (2 * TOK, length), 1)
            scores = jnp.where(col <= row, scores, jnp.float32(-1e30))
            expo = jnp.exp(scores - jnp.max(scores, axis=-1, keepdims=True))
            probs = (expo / jnp.sum(expo, axis=-1, keepdims=True)).astype(jnp.bfloat16)
            out = jnp.dot(
                probs, v_all[0:count].reshape(length, HEAD_SIZE), preferred_element_type=jnp.float32
            ).astype(jnp.bfloat16)
            att[block * TOK : (block + 1) * TOK, cols] = jnp.concatenate(
                [out[:TOK], out[TOK:]], axis=1
            )
            return carry

        lax.fori_loop(0, 4, heads, 0)

    attend(0)
    attend(1)
    attend(2)
    arrive(1)
    arrive(3)
    attend(3)

    across = (z + 2) % 4

    def block_of(i):
        near = i // 9 == 0
        r = i % 9
        q = r // 4
        skip = lambda v: v + v // 2
        a = jnp.where(near, skip(r // 3), 2 * (1 - q) + q * skip(r % 4))
        b = jnp.where(near, skip(r % 3), (r % 4) * (1 - q) + 2 * q)
        return ((x + a) % 4) * 4 + (y + b) % 4

    def project(i, carry):
        j, odd = block_of(i), i % 2
        part[j] = (
            jnp.dot(att[...], w_all[j].reshape(2 * 512, WIDE), preferred_element_type=jnp.float32)
            .astype(jnp.bfloat16)
            .reshape(ZS, TOK, WIDE)
        )
        onward, straight = (z + 1 + 2 * odd) % 4, (z + 3 - 2 * odd) % 4
        remote(
            part.at[j, across], relay.at[j], rs_send, relay_recv.at[j], (onward * 2 + c, ep)
        )
        remote(
            part.at[j, straight],
            final.at[1 - odd, j],
            rs_send,
            final_recv.at[1 - odd, j],
            (straight * 2 + c, ep),
        )
        return carry

    def pass_on(i, carry):
        j, odd = block_of(i), i % 2
        onward = (z + 1 + 2 * odd) % 4
        settle(relay.at[j], relay_recv.at[j])
        part[j, onward] = (
            part[j, onward].astype(jnp.float32) + relay[j].astype(jnp.float32)
        ).astype(jnp.bfloat16)
        remote(
            part.at[j, onward],
            final.at[odd, j],
            rs_send,
            final_recv.at[odd, j],
            (onward * 2 + c, ep),
        )
        return carry

    for d in (0, 1, 3):
        settle(w_all.at[pl.ds(0, 4), 0], wd_recv.at[d])
    lax.fori_loop(0, 9, project, 0)
    lax.fori_loop(0, 9, pass_on, 0)
    arrive(2)
    settle(w_all.at[pl.ds(0, 4), 0], wd_recv.at[2])
    lax.fori_loop(9, BLOCKS, project, 0)
    lax.fori_loop(9, BLOCKS, pass_on, 0)

    def finish(j, squares):
        for side in range(2):
            settle(final.at[side, j], final_recv.at[side, j])
        cols = pl.ds(pl.multiple_of(j * WIDE, WIDE), WIDE)
        total = held[:, cols].astype(jnp.float32) + part[j, z].astype(jnp.float32)
        total = total + final[0, j].astype(jnp.float32) + final[1, j].astype(jnp.float32)
        mixed = total.astype(jnp.bfloat16)
        mixed_ref[:, cols] = mixed
        wide = mixed.astype(jnp.float32)
        wide = wide * wide
        return squares + wide[:, :LANES] + wide[:, LANES:]

    settle(held, held_sem)
    squares = lax.fori_loop(0, BLOCKS, finish, jnp.zeros((TOK, LANES), jnp.float32))
    inverse = lax.rsqrt(jnp.sum(squares, axis=-1, keepdims=True) * np.float32(1.0 / D) + 1e-06)

    def norm(j, carry):
        cols = pl.ds(pl.multiple_of(j * WIDE, WIDE), WIDE)
        normed_ref[:, cols] = (
            mixed_ref[:, cols].astype(jnp.float32) * inverse * gain_ref[:, cols]
        ).astype(jnp.bfloat16)
        return carry

    lax.fori_loop(0, BLOCKS, norm, 0)

    settle(q_all.at[pl.ds(0, 3)], q_send)
    settle(k_all.at[pl.ds(0, 7)], k_send)
    settle(v_all.at[pl.ds(0, 7)], v_send)
    for i in range(2):
        settle(w_all.at[pl.ds(0, 3), 0, top], w1_send.at[i])
        settle(w_all.at[pl.ds(0, 6), 0], w2_send.at[i])
    settle(w_all.at[pl.ds(0, 16), 0], wd_send)
    settle(part.at[:, pl.ds(0, 3)], rs_send)


def mix(queries, keys, values, out_weight, hidden, gain):
    bf16 = jnp.bfloat16
    vmem = pl.BlockSpec(memory_space=pltpu.VMEM)
    anywhere = pl.BlockSpec(memory_space=pl.ANY)
    dma = pltpu.SemaphoreType.DMA
    shape = jax.ShapeDtypeStruct((TOK, D), bf16)
    return pl.pallas_call(
        mix_kernel,
        out_shape=(shape, shape),
        in_specs=[anywhere, vmem, vmem, vmem, anywhere, vmem],
        out_specs=(vmem, vmem),
        scratch_shapes=[
            pltpu.VMEM((ZS, TOK, HEAD_BLOCK), bf16),
            pltpu.VMEM((8, TOK, HEAD_SIZE), bf16),
            pltpu.VMEM((8, TOK, HEAD_SIZE), bf16),
            pltpu.VMEM((BLOCKS, 2, 512, WIDE), bf16),
            pltpu.VMEM((ZS * TOK, HEAD_BLOCK), bf16),
            pltpu.VMEM((BLOCKS, ZS, TOK, WIDE), bf16),
            pltpu.VMEM((BLOCKS, TOK, WIDE), bf16),
            pltpu.VMEM((2, BLOCKS, TOK, WIDE), bf16),
            pltpu.VMEM((TOK, D), bf16),
            dma,
            dma((ZS,)),
            dma,
            dma,
            dma,
            dma,
            dma((2,)),
            dma((2,)),
            dma((2,)),
            dma((2, 4)),
            dma,
            dma((4,)),
            dma,
            dma((BLOCKS,)),
            dma((2, BLOCKS)),
            dma,
        ],
        compiler_params=pltpu.CompilerParams(
            collective_id=1, has_side_effects=True, vmem_limit_bytes=48 * 2**20
        ),
        name="mix",
    )(queries, keys, values, out_weight, hidden, gain)


def body(
    hidden_in,
    queries,
    keys,
    values,
    out_weight,
    norm_gain,
    gate_weight,
    up_weight,
    down_weight,
    expert_ids,
    gates,
    cotangent,
):
    tok = queries.shape[1]
    mixed, normed = mix(
        queries[0], keys[0], values[0], out_weight, hidden_in[0], norm_gain.reshape(1, D)
    )
    row_of, token_of = routes(expert_ids[0])
    three = lambda a: a.reshape(tok, FEATS, LANES)
    out, grads = run_experts(
        token_of,
        row_of,
        gates[0].reshape(-1),
        three(normed),
        three(mixed),
        three(cotangent[0]),
        gate_weight[0],
        up_weight[0],
        down_weight[0],
    )
    return (out[None], jnp.sum(grads, axis=-1)[None])


def solution(mesh):
    placed = (
        P("ep", "sp", None),
        P("ep", "sp", None),
        P("ep", "sp", None),
        P("ep", "sp", None),
        P("sp", "ep"),
        P(),
        P(("sp", "ep"), None, None),
        P(("sp", "ep"), None, None),
        P(("sp", "ep"), None, None),
        P("ep", "sp", None),
        P("ep", "sp", None),
        P("ep", "sp", None),
    )
    return jax.shard_map(
        body,
        mesh=mesh,
        in_specs=placed,
        out_specs=(P("ep", "sp", None), P("ep", "sp", None)),
        check_vma=False,
    )
```

```python
import jax
import jax.numpy as jnp
import numpy as np
from jax import lax
from jax.experimental import pallas as pl
from jax.experimental.pallas import tpu as pltpu
from jax.sharding import PartitionSpec as P

D = 4096
HEAD_SIZE = 128
TOP = 8


MESH = pl.DeviceIdType.MESH
CAP = 9
DEVICES = 128
ROWS = DEVICES * CAP
GROUPS = 8
GROUP_SLOTS = DEVICES // GROUPS
GROUP_ROWS = GROUP_SLOTS * CAP
FFW = 768
LANES = 128
FEATS = D // LANES


def offset_of(step):
    j = (step * (step + 1) // 2) % DEVICES
    return (j // 16) % 4, j // 64, (j // 4) % 4, j % 4


def place():
    sp, ep = lax.axis_index("sp"), lax.axis_index("ep")
    return sp // 2, sp % 2, ep // 4, ep % 4


def target_of(step):
    z, c, x, y = place()
    dz, dc, dx, dy = offset_of(step)
    turn = 1 - 2 * c
    return (
        ((z + turn * dz + 4) % 4) * 2 + (c + dc) % 2,
        ((x + turn * dx + 4) % 4) * 4 + (y + turn * dy + 4) % 4,
    )


def source_of(step):
    z, c, x, y = place()
    dz, dc, dx, dy = offset_of(step)
    core = (c + dc) % 2
    turn = 1 - 2 * core
    return (
        ((z - turn * dz + 4) % 4) * 2 + core,
        ((x - turn * dx + 4) % 4) * 4 + (y - turn * dy + 4) % 4,
    )


def chunk(step):
    return pl.ds(step * CAP, CAP)


def expert_kernel(
    token_ref,
    row_ref,
    scale_ref,
    normed_ref,
    mixed_flat,
    cot_hbm,
    gate_hbm,
    up_hbm,
    down_hbm,
    out_ref,
    grad_ref,
    back_ref,
    gate_w,
    up_w,
    down_w,
    send,
    recv,
    rows,
    inner,
    wide,
    flat,
    mixed_ref,
    cot_ref,
    flat_sem,
    weight_sem,
    send_sem,
    recv_sem,
    out_sem,
    back_sem,
):
    weights = [
        pltpu.make_async_copy(src, dst, weight_sem.at[i])
        for i, (src, dst) in enumerate(((gate_hbm, gate_w), (up_hbm, up_w), (down_hbm, down_w)))
    ]
    for copy in weights:
        copy.start()

    flat_copy = pltpu.make_async_copy(cot_hbm, flat, flat_sem)
    flat_copy.start()

    barrier = pltpu.get_barrier_semaphore()

    def greet(step, carry):
        pl.semaphore_signal(barrier, inc=1, device_id=target_of(step), device_id_type=MESH)
        return carry

    lax.fori_loop(1, DEVICES, greet, 0)

    def fill(step):
        for slot in range(CAP):
            row = step * CAP + slot
            send[row] = normed_ref[token_ref[row]]

    fill(0)
    pl.semaphore_wait(barrier, DEVICES - 1)
    pltpu.make_async_copy(send.at[chunk(0)], recv.at[chunk(0)], recv_sem.at[0]).start()

    def dispatch(step, carry):
        fill(step)
        pltpu.make_async_remote_copy(
            src_ref=send.at[chunk(step)],
            dst_ref=recv.at[chunk(step)],
            send_sem=send_sem,
            recv_sem=recv_sem.at[step // GROUP_SLOTS],
            device_id=target_of(step),
            device_id_type=MESH,
        ).start()
        return carry

    lax.fori_loop(1, DEVICES, dispatch, 0)

    def fold(src, dst):
        def turn(i, carry):
            for f in range(FEATS):
                wide[pl.ds(f, 16, stride=FEATS), :] = src[
                    pl.ds(pl.multiple_of(i * 16, 16), 16), f * LANES : (f + 1) * LANES
                ].astype(jnp.float32)
            dst[pl.ds(i * 16, 16)] = (
                wide[pl.ds(0, 16 * FEATS), :].reshape(16, FEATS, LANES).astype(jnp.bfloat16)
            )
            return carry

        lax.fori_loop(0, src.shape[0] // 16, turn, 0)

    fold(mixed_flat, mixed_ref)
    flat_copy.wait()
    fold(flat, cot_ref)
    for copy in weights:
        copy.wait()

    def work(group, carry):
        base = group * GROUP_ROWS
        block = pl.ds(base, GROUP_ROWS)
        pltpu.make_async_copy(recv.at[block], recv.at[block], recv_sem.at[group]).wait()

        def turn_in(i, carry):
            wide[pl.ds(0, 16 * FEATS), :] = (
                recv[pl.ds(base + i * 16, 16)].astype(jnp.float32).reshape(16 * FEATS, LANES)
            )
            for f in range(FEATS):
                rows[pl.ds(pl.multiple_of(i * 16, 16), 16), f * LANES : (f + 1) * LANES] = wide[
                    pl.ds(f, 16, stride=FEATS), :
                ].astype(jnp.bfloat16)
            return carry

        lax.fori_loop(0, GROUP_ROWS // 16, turn_in, 0)

        def hidden(n, carry):
            cols = pl.ds(pl.multiple_of(n * 256, 256), 256)
            gate_part = jnp.dot(rows[...], gate_w[:, cols], preferred_element_type=jnp.float32)
            up_part = jnp.dot(rows[...], up_w[:, cols], preferred_element_type=jnp.float32)
            inner[:, cols] = (gate_part / (1.0 + jnp.exp(-gate_part)) * up_part).astype(
                jnp.bfloat16
            )
            return carry

        lax.fori_loop(0, FFW // 256, hidden, 0)

        def project(n, carry):
            part = jnp.dot(
                inner[...],
                down_w[:, pl.ds(pl.multiple_of(n * 512, 512), 512)],
                preferred_element_type=jnp.float32,
            )
            for j in range(4):
                wide[pl.ds(n * 4 + j, GROUP_ROWS, stride=FEATS), :] = part[
                    :, j * LANES : (j + 1) * LANES
                ]
            return carry

        lax.fori_loop(0, D // 512, project, 0)

        def turn_out(i, carry):
            part = wide[pl.ds(pl.multiple_of(i * 16 * FEATS, 16 * FEATS), 16 * FEATS), :]
            recv[pl.ds(base + i * 16, 16)] = part.reshape(16, FEATS, LANES).astype(jnp.bfloat16)
            return carry

        lax.fori_loop(0, GROUP_ROWS // 16, turn_out, 0)

        def give_back(step, carry):
            pltpu.make_async_remote_copy(
                src_ref=recv.at[chunk(step)],
                dst_ref=back_ref.at[chunk(step)],
                send_sem=out_sem,
                recv_sem=back_sem,
                device_id=source_of(step),
                device_id_type=MESH,
            ).start()
            return carry

        @pl.when(group == 0)
        def _():
            pltpu.make_async_copy(recv.at[chunk(0)], back_ref.at[chunk(0)], back_sem).start()

        lax.fori_loop(
            jnp.maximum(group * GROUP_SLOTS, 1), (group + 1) * GROUP_SLOTS, give_back, 0
        )
        return carry

    lax.fori_loop(0, GROUPS, work, 0)
    far = pl.ds(CAP, ROWS - CAP)
    pltpu.make_async_copy(send.at[far], send.at[far], send_sem).wait()
    pltpu.make_async_copy(recv.at[far], recv.at[far], out_sem).wait()
    pltpu.make_async_copy(back_ref, back_ref, back_sem).wait()

    def combine(t, carry):
        cot = cot_ref[t].astype(jnp.float32)
        total = mixed_ref[t].astype(jnp.float32)
        sums = []
        for k in range(TOP):
            row = back_ref[row_ref[t * TOP + k]].astype(jnp.float32)
            total = total + scale_ref[t, k] * row
            sums.append(jnp.sum(cot * row, axis=0, keepdims=True))
        out_ref[t] = total.astype(jnp.bfloat16)
        grad_ref[t] = jnp.concatenate(sums, axis=0)
        return carry

    lax.fori_loop(0, out_ref.shape[0], combine, 0)


def run_experts(
    token_of, row_of, gates, normed, mixed, cotangent, gate_weight, up_weight, down_weight
):
    bf16 = jnp.bfloat16
    tok = normed.shape[0]
    anywhere = pl.BlockSpec(memory_space=pl.ANY)
    smem = pl.BlockSpec(memory_space=pltpu.SMEM)
    vmem = pl.BlockSpec(memory_space=pltpu.VMEM)
    return pl.pallas_call(
        expert_kernel,
        out_shape=(
            jax.ShapeDtypeStruct((tok, FEATS, LANES), bf16),
            jax.ShapeDtypeStruct((tok, TOP, LANES), jnp.float32),
        ),
        in_specs=[smem, smem, smem, vmem, vmem, anywhere, anywhere, anywhere, anywhere],
        out_specs=(vmem, vmem),
        scratch_shapes=[
            pltpu.VMEM((ROWS, FEATS, LANES), bf16),
            pltpu.VMEM((D, FFW), bf16),
            pltpu.VMEM((D, FFW), bf16),
            pltpu.VMEM((FFW, D), bf16),
            pltpu.VMEM((ROWS, FEATS, LANES), bf16),
            pltpu.VMEM((ROWS, FEATS, LANES), bf16),
            pltpu.VMEM((GROUP_ROWS, D), bf16),
            pltpu.VMEM((GROUP_ROWS, FFW), bf16),
            pltpu.VMEM((GROUP_ROWS * FEATS, LANES), jnp.float32),
            pltpu.VMEM((tok, D), bf16),
            pltpu.VMEM((tok, FEATS, LANES), bf16),
            pltpu.VMEM((tok, FEATS, LANES), bf16),
            pltpu.SemaphoreType.DMA,
            pltpu.SemaphoreType.DMA((3,)),
            pltpu.SemaphoreType.DMA,
            pltpu.SemaphoreType.DMA((GROUPS,)),
            pltpu.SemaphoreType.DMA,
            pltpu.SemaphoreType.DMA,
        ],
        compiler_params=pltpu.CompilerParams(
            collective_id=0, has_side_effects=True, vmem_limit_bytes=58 * 2**20
        ),
        name="experts",
    )(token_of, row_of, gates, normed, mixed, cotangent, gate_weight, up_weight, down_weight)


def routes(ids):
    flat = ids.reshape(-1)
    sp, ep = target_of(jnp.arange(DEVICES, dtype=jnp.int32))
    named = (sp * 16 + ep)[:, None] == jnp.arange(DEVICES, dtype=jnp.int32)[None, :]
    step_of = jnp.sum(named * jnp.arange(DEVICES, dtype=jnp.int32)[:, None], axis=0)
    onehot = (flat[:, None] == jnp.arange(DEVICES, dtype=jnp.int32)[None, :]).astype(jnp.int32)
    place_of = step_of[None, :] * CAP + jnp.cumsum(onehot, axis=0) - 1
    row_of = jnp.sum(place_of * onehot, axis=1)
    token = jnp.arange(flat.shape[0], dtype=jnp.int32) // TOP
    held = row_of[:, None] == jnp.arange(ROWS, dtype=jnp.int32)[None, :]
    token_of = jnp.sum(jnp.where(held, token[:, None], 0), axis=0)
    return row_of.astype(jnp.int32), token_of.astype(jnp.int32)


HEAD_BLOCK = 8 * HEAD_SIZE
TOK = 128
ZS = 4
WIDE = 256
BLOCKS = D // WIDE
HALF = 256


def mix_kernel(
    query_ref,
    key_ref,
    value_ref,
    weight_ref,
    hidden_ref,
    gain_ref,
    mixed_ref,
    normed_ref,
    q_all,
    k_all,
    v_all,
    w_all,
    att,
    part,
    relay,
    final,
    held,
    q_send,
    q_recv,
    k_send,
    k_recv,
    v_send,
    v_recv,
    w1_send,
    w1_recv,
    w2_send,
    w2_recv,
    wd_send,
    wd_recv,
    rs_send,
    relay_recv,
    final_recv,
    held_sem,
):
    z, c, x, y = place()
    sp, ep = z * 2 + c, x * 4 + y

    def remote(src, dst, send_sem, recv_sem, to):
        pltpu.make_async_remote_copy(
            src_ref=src,
            dst_ref=dst,
            send_sem=send_sem,
            recv_sem=recv_sem,
            device_id=to,
            device_id_type=MESH,
        ).start()

    def local(src, dst, sem):
        pltpu.make_async_copy(src, dst, sem).start()

    def settle(ref, sem):
        pltpu.make_async_copy(ref, ref, sem).wait()

    local(hidden_ref, held, held_sem)
    barrier = pltpu.get_barrier_semaphore()
    for d in range(1, 8):
        pl.semaphore_signal(barrier, inc=1, device_id=((sp + d) % 8, ep), device_id_type=MESH)
    for d in range(1, 4):
        along_x, along_y = (sp, ((x + d) % 4) * 4 + y), (sp, x * 4 + (y + d) % 4)
        pl.semaphore_signal(barrier, inc=1, device_id=along_x, device_id_type=MESH)
        pl.semaphore_signal(barrier, inc=1, device_id=along_y, device_id_type=MESH)
    pl.semaphore_wait(barrier, 13)

    def group_of(other):
        return pl.ds(pl.multiple_of(other // 4 * HEAD_SIZE, HEAD_SIZE), HEAD_SIZE)

    def heads_of(chip):
        return pl.ds(pl.multiple_of(chip * HEAD_BLOCK, HEAD_BLOCK), HEAD_BLOCK)

    top, low = pl.ds(0, HALF), pl.ds(HALF, HALF)
    for d in range(1, 8):
        other = (sp + d) % 8
        remote(key_ref.at[:, group_of(other)], k_all.at[sp], k_send, k_recv, (other, ep))
        remote(value_ref.at[:, group_of(other)], v_all.at[sp], v_send, v_recv, (other, ep))
    for d in range(1, 4):
        along_x, along_y = (sp, ((x + d) % 4) * 4 + y), (sp, x * 4 + (y + d) % 4)
        remote(weight_ref.at[top], w_all.at[ep, c, top], w1_send.at[0], w1_recv.at[0], along_x)
        remote(weight_ref.at[low], w_all.at[ep, c, low], w1_send.at[1], w1_recv.at[1], along_y)
    for d in (1, 3, 2):
        chip = (z + d) % 4
        remote(
            query_ref.at[:, heads_of(chip)], q_all.at[z], q_send, q_recv.at[z], (chip * 2 + c, ep)
        )
    local(key_ref.at[:, group_of(sp)], k_all.at[sp], k_recv)
    local(value_ref.at[:, group_of(sp)], v_all.at[sp], v_recv)
    local(query_ref.at[:, heads_of(z)], q_all.at[z], q_recv.at[z])
    local(weight_ref.at[top], w_all.at[ep, c, top], w1_recv.at[0])
    local(weight_ref.at[low], w_all.at[ep, c, low], w1_recv.at[1])

    settle(w_all.at[pl.ds(0, 2), 0], w1_recv.at[0])
    settle(w_all.at[pl.ds(0, 2), 0], w1_recv.at[1])
    twin = (z * 2 + 1 - c, ep)

    def second(d):
        def send(k, carry):
            mine = w_all.at[k * 4 + y, c, top]
            remote(mine, mine, w2_send.at[0], w2_recv.at[0, d], (sp, x * 4 + (y + d) % 4))
            mine = w_all.at[x * 4 + k, c, low]
            remote(mine, mine, w2_send.at[1], w2_recv.at[1, d], (sp, ((x + d) % 4) * 4 + y))
            return carry

        lax.fori_loop(0, 4, send, 0)

    second(1)
    second(3)

    def share(d):
        def send(k, carry):
            mine = w_all.at[k * 4 + (y + 4 - d) % 4, c, top]
            remote(mine, mine, wd_send, wd_recv.at[d], twin)
            mine = w_all.at[((x + 4 - d) % 4) * 4 + k, c, low]
            remote(mine, mine, wd_send, wd_recv.at[d], twin)
            return carry

        lax.fori_loop(0, 4, send, 0)

    def arrive(d):
        settle(w_all.at[pl.ds(0, 2), 0], w2_recv.at[0, d])
        settle(w_all.at[pl.ds(0, 2), 0], w2_recv.at[1, d])
        share(d)

    share(0)

    settle(k_all, k_recv)
    settle(v_all, v_recv)
    scale = np.float32(1.0 / np.sqrt(HEAD_SIZE))

    def attend(block):
        settle(q_all.at[block], q_recv.at[block])
        count = 2 * block + 2
        length = count * TOK

        def heads(pair, carry):
            cols = pl.ds(pl.multiple_of(pair * 256, 256), 256)
            both = q_all[block, :, cols]
            rows = jnp.concatenate([both[:, :HEAD_SIZE], both[:, HEAD_SIZE:]], axis=0)
            scores = (
                lax.dot_general(
                    rows,
                    k_all[0:count].reshape(length, HEAD_SIZE),
                    (((1,), (1,)), ((), ())),
                    preferred_element_type=jnp.float32,
                )
                * scale
            )
            row = lax.broadcasted_iota(jnp.int32, (2 * TOK, length), 0) % TOK + (
                2 * block + c
            ) * TOK
            col = lax.broadcasted_iota(jnp.int32, (2 * TOK, length), 1)
            scores = jnp.where(col <= row, scores, jnp.float32(-1e30))
            expo = jnp.exp(scores - jnp.max(scores, axis=-1, keepdims=True))
            probs = (expo / jnp.sum(expo, axis=-1, keepdims=True)).astype(jnp.bfloat16)
            out = jnp.dot(
                probs, v_all[0:count].reshape(length, HEAD_SIZE), preferred_element_type=jnp.float32
            ).astype(jnp.bfloat16)
            att[block * TOK : (block + 1) * TOK, cols] = jnp.concatenate(
                [out[:TOK], out[TOK:]], axis=1
            )
            return carry

        lax.fori_loop(0, 4, heads, 0)

    attend(0)
    attend(1)
    arrive(1)
    arrive(3)
    second(2)
    attend(2)
    attend(3)

    across = (z + 2) % 4

    def block_of(i):
        near = i // 9 == 0
        r = i % 9
        q = r // 4
        skip = lambda v: v + v // 2
        a = jnp.where(near, skip(r // 3), 2 * (1 - q) + q * skip(r % 4))
        b = jnp.where(near, skip(r % 3), (r % 4) * (1 - q) + 2 * q)
        return ((x + a) % 4) * 4 + (y + b) % 4

    def project(i, carry):
        j, odd = block_of(i), i % 2
        part[j] = (
            jnp.dot(att[...], w_all[j].reshape(2 * 512, WIDE), preferred_element_type=jnp.float32)
            .astype(jnp.bfloat16)
            .reshape(ZS, TOK, WIDE)
        )
        onward, straight = (z + 1 + 2 * odd) % 4, (z + 3 - 2 * odd) % 4
        remote(
            part.at[j, across], relay.at[j], rs_send, relay_recv.at[j], (onward * 2 + c, ep)
        )
        remote(
            part.at[j, straight],
            final.at[1 - odd, j],
            rs_send,
            final_recv.at[1 - odd, j],
            (straight * 2 + c, ep),
        )
        return carry

    def pass_on(i, carry):
        j, odd = block_of(i), i % 2
        onward = (z + 1 + 2 * odd) % 4
        settle(relay.at[j], relay_recv.at[j])
        part[j, onward] = (
            part[j, onward].astype(jnp.float32) + relay[j].astype(jnp.float32)
        ).astype(jnp.bfloat16)
        remote(
            part.at[j, onward],
            final.at[odd, j],
            rs_send,
            final_recv.at[odd, j],
            (onward * 2 + c, ep),
        )
        return carry

    for d in (0, 1, 3):
        settle(w_all.at[pl.ds(0, 4), 0], wd_recv.at[d])
    lax.fori_loop(0, 9, project, 0)
    lax.fori_loop(0, 9, pass_on, 0)
    arrive(2)
    settle(w_all.at[pl.ds(0, 4), 0], wd_recv.at[2])
    lax.fori_loop(9, BLOCKS, project, 0)
    lax.fori_loop(9, BLOCKS, pass_on, 0)

    def finish(j, squares):
        for side in range(2):
            settle(final.at[side, j], final_recv.at[side, j])
        cols = pl.ds(pl.multiple_of(j * WIDE, WIDE), WIDE)
        total = held[:, cols].astype(jnp.float32) + part[j, z].astype(jnp.float32)
        total = total + final[0, j].astype(jnp.float32) + final[1, j].astype(jnp.float32)
        mixed = total.astype(jnp.bfloat16)
        mixed_ref[:, cols] = mixed
        wide = mixed.astype(jnp.float32)
        wide = wide * wide
        return squares + wide[:, :LANES] + wide[:, LANES:]

    settle(held, held_sem)
    squares = lax.fori_loop(0, BLOCKS, finish, jnp.zeros((TOK, LANES), jnp.float32))
    inverse = lax.rsqrt(jnp.sum(squares, axis=-1, keepdims=True) * np.float32(1.0 / D) + 1e-06)

    def norm(j, carry):
        cols = pl.ds(pl.multiple_of(j * WIDE, WIDE), WIDE)
        normed_ref[:, cols] = (
            mixed_ref[:, cols].astype(jnp.float32) * inverse * gain_ref[:, cols]
        ).astype(jnp.bfloat16)
        return carry

    lax.fori_loop(0, BLOCKS, norm, 0)

    settle(q_all.at[pl.ds(0, 3)], q_send)
    settle(k_all.at[pl.ds(0, 7)], k_send)
    settle(v_all.at[pl.ds(0, 7)], v_send)
    for i in range(2):
        settle(w_all.at[pl.ds(0, 3), 0, top], w1_send.at[i])
        settle(w_all.at[pl.ds(0, 6), 0], w2_send.at[i])
    settle(w_all.at[pl.ds(0, 16), 0], wd_send)
    settle(part.at[:, pl.ds(0, 3)], rs_send)


def mix(queries, keys, values, out_weight, hidden, gain):
    bf16 = jnp.bfloat16
    vmem = pl.BlockSpec(memory_space=pltpu.VMEM)
    anywhere = pl.BlockSpec(memory_space=pl.ANY)
    dma = pltpu.SemaphoreType.DMA
    shape = jax.ShapeDtypeStruct((TOK, D), bf16)
    return pl.pallas_call(
        mix_kernel,
        out_shape=(shape, shape),
        in_specs=[anywhere, vmem, vmem, vmem, anywhere, vmem],
        out_specs=(vmem, vmem),
        scratch_shapes=[
            pltpu.VMEM((ZS, TOK, HEAD_BLOCK), bf16),
            pltpu.VMEM((8, TOK, HEAD_SIZE), bf16),
            pltpu.VMEM((8, TOK, HEAD_SIZE), bf16),
            pltpu.VMEM((BLOCKS, 2, 512, WIDE), bf16),
            pltpu.VMEM((ZS * TOK, HEAD_BLOCK), bf16),
            pltpu.VMEM((BLOCKS, ZS, TOK, WIDE), bf16),
            pltpu.VMEM((BLOCKS, TOK, WIDE), bf16),
            pltpu.VMEM((2, BLOCKS, TOK, WIDE), bf16),
            pltpu.VMEM((TOK, D), bf16),
            dma,
            dma((ZS,)),
            dma,
            dma,
            dma,
            dma,
            dma((2,)),
            dma((2,)),
            dma((2,)),
            dma((2, 4)),
            dma,
            dma((4,)),
            dma,
            dma((BLOCKS,)),
            dma((2, BLOCKS)),
            dma,
        ],
        compiler_params=pltpu.CompilerParams(
            collective_id=1, has_side_effects=True, vmem_limit_bytes=48 * 2**20
        ),
        name="mix",
    )(queries, keys, values, out_weight, hidden, gain)


def body(
    hidden_in,
    queries,
    keys,
    values,
    out_weight,
    norm_gain,
    gate_weight,
    up_weight,
    down_weight,
    expert_ids,
    gates,
    cotangent,
):
    tok = queries.shape[1]
    mixed, normed = mix(
        queries[0], keys[0], values[0], out_weight, hidden_in[0], norm_gain.reshape(1, D)
    )
    row_of, token_of = routes(expert_ids[0])
    three = lambda a: a.reshape(tok, FEATS, LANES)
    out, grads = run_experts(
        token_of,
        row_of,
        gates[0],
        three(normed),
        mixed,
        cotangent[0],
        gate_weight[0],
        up_weight[0],
        down_weight[0],
    )
    return (out.reshape(1, tok, D), jnp.sum(grads, axis=-1)[None])


def solution(mesh):
    placed = (
        P("ep", "sp", None),
        P("ep", "sp", None),
        P("ep", "sp", None),
        P("ep", "sp", None),
        P("sp", "ep"),
        P(),
        P(("sp", "ep"), None, None),
        P(("sp", "ep"), None, None),
        P(("sp", "ep"), None, None),
        P("ep", "sp", None),
        P("ep", "sp", None),
        P("ep", "sp", None),
    )
    return jax.shard_map(
        body,
        mesh=mesh,
        in_specs=placed,
        out_specs=(P("ep", "sp", None), P("ep", "sp", None)),
        check_vma=False,
    )
```

```python
import jax
import jax.numpy as jnp
import numpy as np
from jax import lax
from jax.experimental import pallas as pl
from jax.experimental.pallas import tpu as pltpu
from jax.sharding import PartitionSpec as P

D = 4096
HEAD_SIZE = 128
TOP = 8


MESH = pl.DeviceIdType.MESH
CAP = 9
DEVICES = 128
ROWS = DEVICES * CAP
GROUPS = 8
GROUP_SLOTS = DEVICES // GROUPS
GROUP_ROWS = GROUP_SLOTS * CAP
FFW = 768
LANES = 128
FEATS = D // LANES


def offset_of(step):
    j = (step * (step + 1) // 2) % DEVICES
    return (j // 16) % 4, j // 64, (j // 4) % 4, j % 4


def place():
    sp, ep = lax.axis_index("sp"), lax.axis_index("ep")
    return sp // 2, sp % 2, ep // 4, ep % 4


def target_of(step):
    z, c, x, y = place()
    dz, dc, dx, dy = offset_of(step)
    turn = 1 - 2 * c
    return (
        ((z + turn * dz + 4) % 4) * 2 + (c + dc) % 2,
        ((x + turn * dx + 4) % 4) * 4 + (y + turn * dy + 4) % 4,
    )


def source_of(step):
    z, c, x, y = place()
    dz, dc, dx, dy = offset_of(step)
    core = (c + dc) % 2
    turn = 1 - 2 * core
    return (
        ((z - turn * dz + 4) % 4) * 2 + core,
        ((x - turn * dx + 4) % 4) * 4 + (y - turn * dy + 4) % 4,
    )


def chunk(step):
    return pl.ds(step * CAP, CAP)


def expert_kernel(
    token_hbm,
    row_hbm,
    scale_hbm,
    normed_ref,
    mixed_hbm,
    cot_hbm,
    gate_hbm,
    up_hbm,
    down_hbm,
    out_ref,
    grad_ref,
    back_ref,
    gate_w,
    up_w,
    down_w,
    send,
    recv,
    rows,
    inner,
    wide,
    flat,
    mixed_ref,
    cot_ref,
    scale_ref,
    token_ref,
    row_ref,
    flat_sem,
    weight_sem,
    send_sem,
    recv_sem,
    out_sem,
    back_sem,
):
    small = [
        pltpu.make_async_copy(src, dst, flat_sem.at[i])
        for i, (src, dst) in enumerate(
            ((scale_hbm, scale_ref), (row_hbm, row_ref), (cot_hbm, flat))
        )
    ]
    tokens = pltpu.make_async_copy(token_hbm, token_ref, flat_sem.at[4])
    tokens.start()
    weights = [
        pltpu.make_async_copy(src, dst, weight_sem.at[i])
        for i, (src, dst) in enumerate(((gate_hbm, gate_w), (up_hbm, up_w), (down_hbm, down_w)))
    ]
    for copy in weights:
        copy.start()

    for copy in small:
        copy.start()

    barrier = pltpu.get_barrier_semaphore()

    def greet(step, carry):
        pl.semaphore_signal(barrier, inc=1, device_id=target_of(step), device_id_type=MESH)
        return carry

    lax.fori_loop(1, DEVICES, greet, 0)

    def fill(step):
        for slot in range(CAP):
            row = step * CAP + slot
            send[row] = normed_ref[token_ref[step, slot]]

    tokens.wait()
    fill(0)
    pl.semaphore_wait(barrier, DEVICES - 1)
    pltpu.make_async_copy(send.at[chunk(0)], recv.at[chunk(0)], recv_sem.at[0]).start()

    def dispatch(step, carry):
        fill(step)
        pltpu.make_async_remote_copy(
            src_ref=send.at[chunk(step)],
            dst_ref=recv.at[chunk(step)],
            send_sem=send_sem,
            recv_sem=recv_sem.at[step // GROUP_SLOTS],
            device_id=target_of(step),
            device_id_type=MESH,
        ).start()
        return carry

    lax.fori_loop(1, DEVICES, dispatch, 0)

    def fold(src, dst):
        def turn(i, carry):
            for f in range(FEATS):
                wide[pl.ds(f, 16, stride=FEATS), :] = src[
                    pl.ds(pl.multiple_of(i * 16, 16), 16), f * LANES : (f + 1) * LANES
                ].astype(jnp.float32)
            dst[pl.ds(i * 16, 16)] = (
                wide[pl.ds(0, 16 * FEATS), :].reshape(16, FEATS, LANES).astype(jnp.bfloat16)
            )
            return carry

        lax.fori_loop(0, src.shape[0] // 16, turn, 0)

    for copy in weights:
        copy.wait()

    def work(group, carry):
        base = group * GROUP_ROWS
        block = pl.ds(base, GROUP_ROWS)
        pltpu.make_async_copy(recv.at[block], recv.at[block], recv_sem.at[group]).wait()

        def turn_in(i, carry):
            wide[pl.ds(0, 16 * FEATS), :] = (
                recv[pl.ds(base + i * 16, 16)].astype(jnp.float32).reshape(16 * FEATS, LANES)
            )
            for f in range(FEATS):
                rows[pl.ds(pl.multiple_of(i * 16, 16), 16), f * LANES : (f + 1) * LANES] = wide[
                    pl.ds(f, 16, stride=FEATS), :
                ].astype(jnp.bfloat16)
            return carry

        lax.fori_loop(0, GROUP_ROWS // 16, turn_in, 0)

        def hidden(n, carry):
            cols = pl.ds(pl.multiple_of(n * 256, 256), 256)
            gate_part = jnp.dot(rows[...], gate_w[:, cols], preferred_element_type=jnp.float32)
            up_part = jnp.dot(rows[...], up_w[:, cols], preferred_element_type=jnp.float32)
            inner[:, cols] = (gate_part / (1.0 + jnp.exp(-gate_part)) * up_part).astype(
                jnp.bfloat16
            )
            return carry

        lax.fori_loop(0, FFW // 256, hidden, 0)

        def project(n, carry):
            part = jnp.dot(
                inner[...],
                down_w[:, pl.ds(pl.multiple_of(n * 512, 512), 512)],
                preferred_element_type=jnp.float32,
            )
            for j in range(4):
                wide[pl.ds(n * 4 + j, GROUP_ROWS, stride=FEATS), :] = part[
                    :, j * LANES : (j + 1) * LANES
                ]
            return carry

        lax.fori_loop(0, D // 512, project, 0)

        def turn_out(i, carry):
            part = wide[pl.ds(pl.multiple_of(i * 16 * FEATS, 16 * FEATS), 16 * FEATS), :]
            recv[pl.ds(base + i * 16, 16)] = part.reshape(16, FEATS, LANES).astype(jnp.bfloat16)
            return carry

        lax.fori_loop(0, GROUP_ROWS // 16, turn_out, 0)

        def give_back(step, carry):
            pltpu.make_async_remote_copy(
                src_ref=recv.at[chunk(step)],
                dst_ref=back_ref.at[chunk(step)],
                send_sem=out_sem,
                recv_sem=back_sem,
                device_id=source_of(step),
                device_id_type=MESH,
            ).start()
            return carry

        @pl.when(group == 0)
        def _():
            pltpu.make_async_copy(recv.at[chunk(0)], back_ref.at[chunk(0)], back_sem).start()

        lax.fori_loop(
            jnp.maximum(group * GROUP_SLOTS, 1), (group + 1) * GROUP_SLOTS, give_back, 0
        )
        return carry

    lax.fori_loop(0, GROUPS, work, 0)
    for copy in small:
        copy.wait()
    fold(flat, cot_ref)
    last = pltpu.make_async_copy(mixed_hbm, flat, flat_sem.at[3])
    last.start()
    last.wait()
    fold(flat, mixed_ref)
    far = pl.ds(CAP, ROWS - CAP)
    pltpu.make_async_copy(send.at[far], send.at[far], send_sem).wait()
    pltpu.make_async_copy(recv.at[far], recv.at[far], out_sem).wait()
    pltpu.make_async_copy(back_ref, back_ref, back_sem).wait()

    def combine(t, carry):
        cot = cot_ref[t].astype(jnp.float32)
        total = mixed_ref[t].astype(jnp.float32)
        for k in range(TOP):
            row = back_ref[row_ref[k, t]].astype(jnp.float32)
            total = total + scale_ref[k, t] * row
            grad_ref[k, pl.ds(t, 1), :] = jnp.sum(cot * row, axis=0, keepdims=True)
        out_ref[t] = total.astype(jnp.bfloat16)
        return carry

    lax.fori_loop(0, out_ref.shape[0], combine, 0)


def run_experts(
    token_of, row_of, gates, normed, mixed, cotangent, gate_weight, up_weight, down_weight
):
    bf16 = jnp.bfloat16
    tok = normed.shape[0]
    anywhere = pl.BlockSpec(memory_space=pl.ANY)
    vmem = pl.BlockSpec(memory_space=pltpu.VMEM)
    return pl.pallas_call(
        expert_kernel,
        out_shape=(
            jax.ShapeDtypeStruct((tok, FEATS, LANES), bf16),
            jax.ShapeDtypeStruct((TOP, tok, LANES), jnp.float32),
        ),
        in_specs=[anywhere] * 3 + [vmem] + [anywhere] * 5,
        out_specs=(vmem, vmem),
        scratch_shapes=[
            pltpu.VMEM((ROWS, FEATS, LANES), bf16),
            pltpu.VMEM((D, FFW), bf16),
            pltpu.VMEM((D, FFW), bf16),
            pltpu.VMEM((FFW, D), bf16),
            pltpu.VMEM((ROWS, FEATS, LANES), bf16),
            pltpu.VMEM((ROWS, FEATS, LANES), bf16),
            pltpu.VMEM((GROUP_ROWS, D), bf16),
            pltpu.VMEM((GROUP_ROWS, FFW), bf16),
            pltpu.VMEM((GROUP_ROWS * FEATS, LANES), jnp.float32),
            pltpu.VMEM((tok, D), bf16),
            pltpu.VMEM((tok, FEATS, LANES), bf16),
            pltpu.VMEM((tok, FEATS, LANES), bf16),
            pltpu.SMEM((TOP, tok), jnp.float32),
            pltpu.SMEM((DEVICES, 16), jnp.int32),
            pltpu.SMEM((TOP, tok), jnp.int32),
            pltpu.SemaphoreType.DMA((5,)),
            pltpu.SemaphoreType.DMA((3,)),
            pltpu.SemaphoreType.DMA,
            pltpu.SemaphoreType.DMA((GROUPS,)),
            pltpu.SemaphoreType.DMA,
            pltpu.SemaphoreType.DMA,
        ],
        compiler_params=pltpu.CompilerParams(
            collective_id=0, has_side_effects=True, vmem_limit_bytes=60 * 2**20
        ),
        name="experts",
    )(token_of, row_of, gates, normed, mixed, cotangent, gate_weight, up_weight, down_weight)


def route(ids_ref, row_out, token_out):
    square = (DEVICES, DEVICES)
    down = lax.broadcasted_iota(jnp.int32, square, 0)
    across = lax.broadcasted_iota(jnp.int32, square, 1)
    sp, ep = target_of(across)
    step_of = jnp.sum(jnp.where(sp * 16 + ep == down, across, 0), axis=1, keepdims=True)
    steps = []
    held = jnp.zeros(square, jnp.float32)
    for k in range(TOP):
        named = ids_ref[k : k + 1, :] == down
        step = jnp.sum(jnp.where(named, step_of, 0), axis=0, keepdims=True)
        held = held + jnp.where(step == down, 1.0, 0.0)
        steps.append(step)
    earlier = jnp.where(down < across, 1.0, 0.0).astype(jnp.bfloat16)
    before = jnp.dot(
        held.astype(jnp.bfloat16), earlier, preferred_element_type=jnp.float32
    ).astype(jnp.int32)
    for k in range(TOP):
        place_of = jnp.sum(jnp.where(steps[k] == down, before, 0), axis=0, keepdims=True)
        row_out[k : k + 1, :] = steps[k] * CAP + place_of
    token_out[...] = jnp.zeros_like(token_out)
    for slot in range(CAP):
        fits = jnp.where((held > 0.5) & (before == slot), across, 0)
        token_out[:, slot : slot + 1] = jnp.sum(fits, axis=1, keepdims=True)


HEAD_BLOCK = 8 * HEAD_SIZE
TOK = 128
ZS = 4
WIDE = 256
BLOCKS = D // WIDE
HALF = 256


def mix_kernel(
    query_ref,
    key_ref,
    value_ref,
    weight_ref,
    hidden_ref,
    gain_hbm,
    ids_hbm,
    mixed_out,
    normed_ref,
    row_out,
    token_out,
    q_all,
    k_all,
    v_all,
    w_all,
    att,
    part,
    relay,
    final,
    held,
    mixed_ref,
    ids_ref,
    gain_ref,
    folded,
    q_send,
    q_recv,
    k_send,
    k_recv,
    v_send,
    v_recv,
    w1_send,
    w1_recv,
    w2_send,
    w2_recv,
    wd_send,
    wd_recv,
    rs_send,
    relay_recv,
    final_recv,
    held_sem,
    ids_sem,
    mixed_sem,
    gain_sem,
):
    z, c, x, y = place()
    sp, ep = z * 2 + c, x * 4 + y

    def remote(src, dst, send_sem, recv_sem, to):
        pltpu.make_async_remote_copy(
            src_ref=src,
            dst_ref=dst,
            send_sem=send_sem,
            recv_sem=recv_sem,
            device_id=to,
            device_id_type=MESH,
        ).start()

    def local(src, dst, sem):
        pltpu.make_async_copy(src, dst, sem).start()

    def settle(ref, sem):
        pltpu.make_async_copy(ref, ref, sem).wait()

    local(hidden_ref, held, held_sem)
    local(ids_hbm, ids_ref, ids_sem)
    local(gain_hbm, gain_ref, gain_sem)
    barrier = pltpu.get_barrier_semaphore()
    for d in range(1, 8):
        pl.semaphore_signal(barrier, inc=1, device_id=((sp + d) % 8, ep), device_id_type=MESH)
    for d in range(1, 4):
        along_x, along_y = (sp, ((x + d) % 4) * 4 + y), (sp, x * 4 + (y + d) % 4)
        pl.semaphore_signal(barrier, inc=1, device_id=along_x, device_id_type=MESH)
        pl.semaphore_signal(barrier, inc=1, device_id=along_y, device_id_type=MESH)
    pl.semaphore_wait(barrier, 13)

    def group_of(other):
        return pl.ds(pl.multiple_of(other // 4 * HEAD_SIZE, HEAD_SIZE), HEAD_SIZE)

    def heads_of(chip):
        return pl.ds(pl.multiple_of(chip * HEAD_BLOCK, HEAD_BLOCK), HEAD_BLOCK)

    top, low = pl.ds(0, HALF), pl.ds(HALF, HALF)
    for d in range(1, 8):
        other = (sp + d) % 8
        remote(key_ref.at[:, group_of(other)], k_all.at[sp], k_send, k_recv, (other, ep))
        remote(value_ref.at[:, group_of(other)], v_all.at[sp], v_send, v_recv, (other, ep))
    for d in range(1, 4):
        along_x, along_y = (sp, ((x + d) % 4) * 4 + y), (sp, x * 4 + (y + d) % 4)
        remote(weight_ref.at[top], w_all.at[ep, c, top], w1_send.at[0], w1_recv.at[0], along_x)
        remote(weight_ref.at[low], w_all.at[ep, c, low], w1_send.at[1], w1_recv.at[1], along_y)
    for d in (1, 3, 2):
        chip = (z + d) % 4
        remote(
            query_ref.at[:, heads_of(chip)], q_all.at[z], q_send, q_recv.at[z], (chip * 2 + c, ep)
        )
    local(key_ref.at[:, group_of(sp)], k_all.at[sp], k_recv)
    local(value_ref.at[:, group_of(sp)], v_all.at[sp], v_recv)
    local(query_ref.at[:, heads_of(z)], q_all.at[z], q_recv.at[z])
    local(weight_ref.at[top], w_all.at[ep, c, top], w1_recv.at[0])
    local(weight_ref.at[low], w_all.at[ep, c, low], w1_recv.at[1])

    settle(w_all.at[pl.ds(0, 2), 0], w1_recv.at[0])
    settle(w_all.at[pl.ds(0, 2), 0], w1_recv.at[1])
    twin = (z * 2 + 1 - c, ep)

    def second(d):
        def send(k, carry):
            mine = w_all.at[k * 4 + y, c, top]
            remote(mine, mine, w2_send.at[0], w2_recv.at[0, d], (sp, x * 4 + (y + d) % 4))
            mine = w_all.at[x * 4 + k, c, low]
            remote(mine, mine, w2_send.at[1], w2_recv.at[1, d], (sp, ((x + d) % 4) * 4 + y))
            return carry

        lax.fori_loop(0, 4, send, 0)

    second(1)
    second(3)

    def share(d):
        def send(k, carry):
            mine = w_all.at[k * 4 + (y + 4 - d) % 4, c, top]
            remote(mine, mine, wd_send, wd_recv.at[d], twin)
            mine = w_all.at[((x + 4 - d) % 4) * 4 + k, c, low]
            remote(mine, mine, wd_send, wd_recv.at[d], twin)
            return carry

        lax.fori_loop(0, 4, send, 0)

    def arrive(d):
        settle(w_all.at[pl.ds(0, 2), 0], w2_recv.at[0, d])
        settle(w_all.at[pl.ds(0, 2), 0], w2_recv.at[1, d])
        share(d)

    share(0)

    settle(ids_ref, ids_sem)
    route(ids_ref, row_out, token_out)

    settle(k_all, k_recv)
    settle(v_all, v_recv)
    scale = np.float32(np.log2(np.e) / np.sqrt(HEAD_SIZE))

    def attend(block):
        settle(q_all.at[block], q_recv.at[block])
        past = 2 * block * TOK

        def against(rows, first, length):
            return lax.dot_general(
                rows,
                k_all[first : first + length].reshape(length * TOK, HEAD_SIZE),
                (((1,), (1,)), ((), ())),
                preferred_element_type=jnp.float32,
            )

        def times(probs, first, length):
            return jnp.dot(
                probs.astype(jnp.bfloat16),
                v_all[first : first + length].reshape(length * TOK, HEAD_SIZE),
                preferred_element_type=jnp.float32,
            )

        def heads(pair, carry):
            cols = pl.ds(pl.multiple_of(pair * 256, 256), 256)
            both = q_all[block, :, cols]
            rows = jnp.concatenate([both[:, :HEAD_SIZE], both[:, HEAD_SIZE:]], axis=0)
            near = against(rows, 2 * block, 2)
            row = lax.broadcasted_iota(jnp.int32, near.shape, 0) % TOK + c * TOK
            col = lax.broadcasted_iota(jnp.int32, near.shape, 1)
            near = jnp.where(col <= row, near, jnp.float32(-1e30))
            top = jnp.max(near, axis=-1, keepdims=True)
            if past:
                far = against(rows, 0, 2 * block)
                top = jnp.maximum(top, jnp.max(far, axis=-1, keepdims=True))
            near = jnp.exp2((near - top) * scale)
            total = jnp.sum(near, axis=-1, keepdims=True)
            out = times(near, 2 * block, 2)
            if past:
                far = jnp.exp2((far - top) * scale)
                total = total + jnp.sum(far, axis=-1, keepdims=True)
                out = out + times(far, 0, 2 * block)
            out = (out * (1.0 / total)).astype(jnp.bfloat16)
            att[block * TOK : (block + 1) * TOK, cols] = jnp.concatenate(
                [out[:TOK], out[TOK:]], axis=1
            )
            return carry

        lax.fori_loop(0, 4, heads, 0)

    attend(0)
    attend(1)
    arrive(1)
    arrive(3)
    second(2)
    attend(2)
    attend(3)

    across = (z + 2) % 4

    def block_of(i):
        near = i // 9 == 0
        r = i % 9
        q = r // 4
        skip = lambda v: v + v // 2
        a = jnp.where(near, skip(r // 3), 2 * (1 - q) + q * skip(r % 4))
        b = jnp.where(near, skip(r % 3), (r % 4) * (1 - q) + 2 * q)
        return ((x + a) % 4) * 4 + (y + b) % 4

    def project(i, carry):
        j, odd = block_of(i), i % 2
        part[j] = (
            jnp.dot(att[...], w_all[j].reshape(2 * 512, WIDE), preferred_element_type=jnp.float32)
            .astype(jnp.bfloat16)
            .reshape(ZS, TOK, WIDE)
        )
        onward, straight = (z + 1 + 2 * odd) % 4, (z + 3 - 2 * odd) % 4
        remote(
            part.at[j, across], relay.at[j], rs_send, relay_recv.at[j], (onward * 2 + c, ep)
        )
        remote(
            part.at[j, straight],
            final.at[1 - odd, j],
            rs_send,
            final_recv.at[1 - odd, j],
            (straight * 2 + c, ep),
        )
        return carry

    def pass_on(i, carry):
        j, odd = block_of(i), i % 2
        onward = (z + 1 + 2 * odd) % 4
        settle(relay.at[j], relay_recv.at[j])
        part[j, onward] = (
            part[j, onward].astype(jnp.float32) + relay[j].astype(jnp.float32)
        ).astype(jnp.bfloat16)
        remote(
            part.at[j, onward],
            final.at[odd, j],
            rs_send,
            final_recv.at[odd, j],
            (onward * 2 + c, ep),
        )
        return carry

    for d in (0, 1, 3):
        settle(w_all.at[pl.ds(0, 4), 0], wd_recv.at[d])
    lax.fori_loop(0, 9, project, 0)
    lax.fori_loop(0, 9, pass_on, 0)
    arrive(2)
    settle(w_all.at[pl.ds(0, 4), 0], wd_recv.at[2])
    lax.fori_loop(9, BLOCKS, project, 0)
    lax.fori_loop(9, BLOCKS, pass_on, 0)

    def finish(j, squares):
        for side in range(2):
            settle(final.at[side, j], final_recv.at[side, j])
        cols = pl.ds(pl.multiple_of(j * WIDE, WIDE), WIDE)
        total = held[:, cols].astype(jnp.float32) + part[j, z].astype(jnp.float32)
        total = total + final[0, j].astype(jnp.float32) + final[1, j].astype(jnp.float32)
        mixed = total.astype(jnp.bfloat16)
        mixed_ref[:, cols] = mixed
        wide = mixed.astype(jnp.float32)
        wide = wide * wide
        return squares + wide[:, :LANES] + wide[:, LANES:]

    settle(held, held_sem)
    squares = lax.fori_loop(0, BLOCKS, finish, jnp.zeros((TOK, LANES), jnp.float32))
    local(mixed_ref, mixed_out, mixed_sem)
    inverse = lax.rsqrt(jnp.sum(squares, axis=-1, keepdims=True) * np.float32(1.0 / D) + 1e-06)

    settle(gain_ref, gain_sem)

    def norm(j, carry):
        cols = pl.ds(pl.multiple_of(j * WIDE, WIDE), WIDE)
        normed = mixed_ref[:, cols].astype(jnp.float32) * inverse * gain_ref[:, cols]
        for half in range(WIDE // LANES):
            folded[pl.ds(j * (WIDE // LANES) + half, TOK, stride=FEATS), :] = normed[
                :, half * LANES : (half + 1) * LANES
            ]
        return carry

    lax.fori_loop(0, BLOCKS, norm, 0)

    def narrow(i, carry):
        part = folded[pl.ds(pl.multiple_of(i * 16 * FEATS, 16 * FEATS), 16 * FEATS), :]
        normed_ref[pl.ds(i * 16, 16)] = part.reshape(16, FEATS, LANES).astype(jnp.bfloat16)
        return carry

    lax.fori_loop(0, TOK // 16, narrow, 0)

    settle(mixed_ref, mixed_sem)
    settle(q_all.at[pl.ds(0, 3)], q_send)
    settle(k_all.at[pl.ds(0, 7)], k_send)
    settle(v_all.at[pl.ds(0, 7)], v_send)
    for i in range(2):
        settle(w_all.at[pl.ds(0, 3), 0, top], w1_send.at[i])
        settle(w_all.at[pl.ds(0, 6), 0], w2_send.at[i])
    settle(w_all.at[pl.ds(0, 16), 0], wd_send)
    settle(part.at[:, pl.ds(0, 3)], rs_send)


def mix(queries, keys, values, out_weight, hidden, gain, ids):
    bf16 = jnp.bfloat16
    vmem = pl.BlockSpec(memory_space=pltpu.VMEM)
    anywhere = pl.BlockSpec(memory_space=pl.ANY)
    dma = pltpu.SemaphoreType.DMA
    shape = jax.ShapeDtypeStruct((TOK, D), bf16)
    return pl.pallas_call(
        mix_kernel,
        out_shape=(
            shape,
            jax.ShapeDtypeStruct((TOK, FEATS, LANES), bf16),
            jax.ShapeDtypeStruct((TOP, TOK), jnp.int32),
            jax.ShapeDtypeStruct((DEVICES, 16), jnp.int32),
        ),
        in_specs=[anywhere] * 7,
        out_specs=(anywhere, vmem, vmem, vmem),
        scratch_shapes=[
            pltpu.VMEM((ZS, TOK, HEAD_BLOCK), bf16),
            pltpu.VMEM((8, TOK, HEAD_SIZE), bf16),
            pltpu.VMEM((8, TOK, HEAD_SIZE), bf16),
            pltpu.VMEM((BLOCKS, 2, 512, WIDE), bf16),
            pltpu.VMEM((ZS * TOK, HEAD_BLOCK), bf16),
            pltpu.VMEM((BLOCKS, ZS, TOK, WIDE), bf16),
            pltpu.VMEM((BLOCKS, TOK, WIDE), bf16),
            pltpu.VMEM((2, BLOCKS, TOK, WIDE), bf16),
            pltpu.VMEM((TOK, D), bf16),
            pltpu.VMEM((TOK, D), bf16),
            pltpu.VMEM((TOP, TOK), jnp.int32),
            pltpu.VMEM((1, D), jnp.float32),
            pltpu.VMEM((TOK * FEATS, LANES), jnp.float32),
            dma,
            dma((ZS,)),
            dma,
            dma,
            dma,
            dma,
            dma((2,)),
            dma((2,)),
            dma((2,)),
            dma((2, 4)),
            dma,
            dma((4,)),
            dma,
            dma((BLOCKS,)),
            dma((2, BLOCKS)),
            dma,
            dma,
            dma,
            dma,
        ],
        compiler_params=pltpu.CompilerParams(
            collective_id=1, has_side_effects=True, vmem_limit_bytes=62 * 2**20
        ),
        name="mix",
    )(queries, keys, values, out_weight, hidden, gain, ids)


def body(
    hidden_in,
    queries,
    keys,
    values,
    out_weight,
    norm_gain,
    gate_weight,
    up_weight,
    down_weight,
    expert_ids,
    gates,
    cotangent,
):
    tok = queries.shape[1]
    mixed, normed, row_of, token_of = mix(
        queries[0],
        keys[0],
        values[0],
        out_weight,
        hidden_in[0],
        norm_gain.reshape(1, D),
        expert_ids[0].T,
    )
    out, grads = run_experts(
        token_of,
        row_of,
        gates[0].T,
        normed,
        mixed,
        cotangent[0],
        gate_weight[0],
        up_weight[0],
        down_weight[0],
    )
    return (out.reshape(1, tok, D), jnp.sum(grads, axis=-1).T[None])


def solution(mesh):
    placed = (
        P("ep", "sp", None),
        P("ep", "sp", None),
        P("ep", "sp", None),
        P("ep", "sp", None),
        P("sp", "ep"),
        P(),
        P(("sp", "ep"), None, None),
        P(("sp", "ep"), None, None),
        P(("sp", "ep"), None, None),
        P("ep", "sp", None),
        P("ep", "sp", None),
        P("ep", "sp", None),
    )
    return jax.shard_map(
        body,
        mesh=mesh,
        in_specs=placed,
        out_specs=(P("ep", "sp", None), P("ep", "sp", None)),
        check_vma=False,
    )
```

```python
import jax
import jax.numpy as jnp
import numpy as np
from jax import lax
from jax.experimental import pallas as pl
from jax.experimental.pallas import tpu as pltpu
from jax.sharding import PartitionSpec as P

D = 4096
HEAD_SIZE = 128
TOP = 8


MESH = pl.DeviceIdType.MESH
CAP = 9
DEVICES = 128
ROWS = DEVICES * CAP
GROUPS = 8
GROUP_SLOTS = DEVICES // GROUPS
GROUP_ROWS = GROUP_SLOTS * CAP
FFW = 768
LANES = 128
FEATS = D // LANES


def offset_of(step):
    a, b, c, e = step % 4, (step // 4) % 4, (step // 16) % 4, step // 64
    return (a + b) % 4, (a + b + e) % 2, (3 * a + b + c) % 4, a


def place():
    sp, ep = lax.axis_index("sp"), lax.axis_index("ep")
    return sp // 2, sp % 2, ep // 4, ep % 4


def target_of(step):
    z, c, x, y = place()
    dz, dc, dx, dy = offset_of(step)
    turn = 1 - 2 * c
    return (
        ((z + turn * dz + 4) % 4) * 2 + (c + dc) % 2,
        ((x + turn * dx + 4) % 4) * 4 + (y + turn * dy + 4) % 4,
    )


def source_of(step):
    z, c, x, y = place()
    dz, dc, dx, dy = offset_of(step)
    core = (c + dc) % 2
    turn = 1 - 2 * core
    return (
        ((z - turn * dz + 4) % 4) * 2 + core,
        ((x - turn * dx + 4) % 4) * 4 + (y - turn * dy + 4) % 4,
    )


def chunk(step):
    return pl.ds(step * CAP, CAP)


def expert_kernel(
    token_hbm,
    row_hbm,
    scale_hbm,
    normed_ref,
    mixed_hbm,
    cot_hbm,
    gate_hbm,
    up_hbm,
    down_hbm,
    out_ref,
    grad_ref,
    back_ref,
    gate_w,
    up_w,
    down_w,
    send,
    recv,
    rows,
    inner,
    wide,
    flat,
    mixed_ref,
    cot_ref,
    scale_ref,
    token_ref,
    row_ref,
    flat_sem,
    weight_sem,
    send_sem,
    recv_sem,
    out_sem,
    back_sem,
):
    small = [
        pltpu.make_async_copy(src, dst, flat_sem.at[i])
        for i, (src, dst) in enumerate(
            ((scale_hbm, scale_ref), (row_hbm, row_ref), (cot_hbm, flat))
        )
    ]
    tokens = pltpu.make_async_copy(token_hbm, token_ref, flat_sem.at[4])
    tokens.start()
    weights = [
        pltpu.make_async_copy(src, dst, weight_sem.at[i])
        for i, (src, dst) in enumerate(((gate_hbm, gate_w), (up_hbm, up_w), (down_hbm, down_w)))
    ]
    for copy in weights:
        copy.start()

    for copy in small:
        copy.start()

    barrier = pltpu.get_barrier_semaphore()

    def greet(step, carry):
        pl.semaphore_signal(barrier, inc=1, device_id=target_of(step), device_id_type=MESH)
        return carry

    lax.fori_loop(1, DEVICES, greet, 0)

    def fill(step):
        for slot in range(CAP):
            row = step * CAP + slot
            send[row] = normed_ref[token_ref[step, slot]]

    tokens.wait()
    fill(0)
    pl.semaphore_wait(barrier, DEVICES - 1)
    pltpu.make_async_copy(send.at[chunk(0)], recv.at[chunk(0)], recv_sem.at[0]).start()

    def dispatch(step, carry):
        fill(step)
        pltpu.make_async_remote_copy(
            src_ref=send.at[chunk(step)],
            dst_ref=recv.at[chunk(step)],
            send_sem=send_sem,
            recv_sem=recv_sem.at[step // GROUP_SLOTS],
            device_id=target_of(step),
            device_id_type=MESH,
        ).start()
        return carry

    lax.fori_loop(1, DEVICES, dispatch, 0)

    def fold(src, dst):
        def turn(i, carry):
            for f in range(FEATS):
                wide[pl.ds(f, 16, stride=FEATS), :] = src[
                    pl.ds(pl.multiple_of(i * 16, 16), 16), f * LANES : (f + 1) * LANES
                ].astype(jnp.float32)
            dst[pl.ds(i * 16, 16)] = (
                wide[pl.ds(0, 16 * FEATS), :].reshape(16, FEATS, LANES).astype(jnp.bfloat16)
            )
            return carry

        lax.fori_loop(0, src.shape[0] // 16, turn, 0)

    for copy in weights:
        copy.wait()

    def work(group, carry):
        base = group * GROUP_ROWS
        block = pl.ds(base, GROUP_ROWS)
        pltpu.make_async_copy(recv.at[block], recv.at[block], recv_sem.at[group]).wait()

        def turn_in(i, carry):
            wide[pl.ds(0, 16 * FEATS), :] = (
                recv[pl.ds(base + i * 16, 16)].astype(jnp.float32).reshape(16 * FEATS, LANES)
            )
            for f in range(FEATS):
                rows[pl.ds(pl.multiple_of(i * 16, 16), 16), f * LANES : (f + 1) * LANES] = wide[
                    pl.ds(f, 16, stride=FEATS), :
                ].astype(jnp.bfloat16)
            return carry

        lax.fori_loop(0, GROUP_ROWS // 16, turn_in, 0)

        def hidden(n, carry):
            cols = pl.ds(pl.multiple_of(n * 256, 256), 256)
            gate_part = jnp.dot(rows[...], gate_w[:, cols], preferred_element_type=jnp.float32)
            up_part = jnp.dot(rows[...], up_w[:, cols], preferred_element_type=jnp.float32)
            inner[:, cols] = (gate_part / (1.0 + jnp.exp(-gate_part)) * up_part).astype(
                jnp.bfloat16
            )
            return carry

        lax.fori_loop(0, FFW // 256, hidden, 0)

        def project(n, carry):
            part = jnp.dot(
                inner[...],
                down_w[:, pl.ds(pl.multiple_of(n * 512, 512), 512)],
                preferred_element_type=jnp.float32,
            )
            for j in range(4):
                wide[pl.ds(n * 4 + j, GROUP_ROWS, stride=FEATS), :] = part[
                    :, j * LANES : (j + 1) * LANES
                ]
            return carry

        lax.fori_loop(0, D // 512, project, 0)

        def turn_out(i, carry):
            part = wide[pl.ds(pl.multiple_of(i * 16 * FEATS, 16 * FEATS), 16 * FEATS), :]
            recv[pl.ds(base + i * 16, 16)] = part.reshape(16, FEATS, LANES).astype(jnp.bfloat16)
            return carry

        lax.fori_loop(0, GROUP_ROWS // 16, turn_out, 0)

        def give_back(step, carry):
            pltpu.make_async_remote_copy(
                src_ref=recv.at[chunk(step)],
                dst_ref=back_ref.at[chunk(step)],
                send_sem=out_sem,
                recv_sem=back_sem,
                device_id=source_of(step),
                device_id_type=MESH,
            ).start()
            return carry

        @pl.when(group == 0)
        def _():
            pltpu.make_async_copy(recv.at[chunk(0)], back_ref.at[chunk(0)], back_sem).start()

        lax.fori_loop(
            jnp.maximum(group * GROUP_SLOTS, 1), (group + 1) * GROUP_SLOTS, give_back, 0
        )
        return carry

    lax.fori_loop(0, GROUPS, work, 0)
    for copy in small:
        copy.wait()
    fold(flat, cot_ref)
    last = pltpu.make_async_copy(mixed_hbm, flat, flat_sem.at[3])
    last.start()
    last.wait()
    fold(flat, mixed_ref)
    far = pl.ds(CAP, ROWS - CAP)
    pltpu.make_async_copy(send.at[far], send.at[far], send_sem).wait()
    pltpu.make_async_copy(recv.at[far], recv.at[far], out_sem).wait()
    pltpu.make_async_copy(back_ref, back_ref, back_sem).wait()

    def combine(t, carry):
        cot = cot_ref[t].astype(jnp.float32)
        total = mixed_ref[t].astype(jnp.float32)
        for k in range(TOP):
            row = back_ref[row_ref[k, t]].astype(jnp.float32)
            total = total + scale_ref[k, t] * row
            grad_ref[k, pl.ds(t, 1), :] = jnp.sum(cot * row, axis=0, keepdims=True)
        out_ref[t] = total.astype(jnp.bfloat16)
        return carry

    lax.fori_loop(0, out_ref.shape[0], combine, 0)


def run_experts(
    token_of, row_of, gates, normed, mixed, cotangent, gate_weight, up_weight, down_weight
):
    bf16 = jnp.bfloat16
    tok = normed.shape[0]
    anywhere = pl.BlockSpec(memory_space=pl.ANY)
    vmem = pl.BlockSpec(memory_space=pltpu.VMEM)
    return pl.pallas_call(
        expert_kernel,
        out_shape=(
            jax.ShapeDtypeStruct((tok, FEATS, LANES), bf16),
            jax.ShapeDtypeStruct((TOP, tok, LANES), jnp.float32),
        ),
        in_specs=[anywhere] * 3 + [vmem] + [anywhere] * 5,
        out_specs=(vmem, vmem),
        scratch_shapes=[
            pltpu.VMEM((ROWS, FEATS, LANES), bf16),
            pltpu.VMEM((D, FFW), bf16),
            pltpu.VMEM((D, FFW), bf16),
            pltpu.VMEM((FFW, D), bf16),
            pltpu.VMEM((ROWS, FEATS, LANES), bf16),
            pltpu.VMEM((ROWS, FEATS, LANES), bf16),
            pltpu.VMEM((GROUP_ROWS, D), bf16),
            pltpu.VMEM((GROUP_ROWS, FFW), bf16),
            pltpu.VMEM((GROUP_ROWS * FEATS, LANES), jnp.float32),
            pltpu.VMEM((tok, D), bf16),
            pltpu.VMEM((tok, FEATS, LANES), bf16),
            pltpu.VMEM((tok, FEATS, LANES), bf16),
            pltpu.SMEM((TOP, tok), jnp.float32),
            pltpu.SMEM((DEVICES, 16), jnp.int32),
            pltpu.SMEM((TOP, tok), jnp.int32),
            pltpu.SemaphoreType.DMA((5,)),
            pltpu.SemaphoreType.DMA((3,)),
            pltpu.SemaphoreType.DMA,
            pltpu.SemaphoreType.DMA((GROUPS,)),
            pltpu.SemaphoreType.DMA,
            pltpu.SemaphoreType.DMA,
        ],
        compiler_params=pltpu.CompilerParams(
            collective_id=0, has_side_effects=True, vmem_limit_bytes=60 * 2**20
        ),
        name="experts",
    )(token_of, row_of, gates, normed, mixed, cotangent, gate_weight, up_weight, down_weight)


def route(ids_ref, row_out, token_out):
    square = (DEVICES, DEVICES)
    down = lax.broadcasted_iota(jnp.int32, square, 0)
    across = lax.broadcasted_iota(jnp.int32, square, 1)
    sp, ep = target_of(across)
    step_of = jnp.sum(jnp.where(sp * 16 + ep == down, across, 0), axis=1, keepdims=True)
    steps = []
    held = jnp.zeros(square, jnp.float32)
    for k in range(TOP):
        named = ids_ref[k : k + 1, :] == down
        step = jnp.sum(jnp.where(named, step_of, 0), axis=0, keepdims=True)
        held = held + jnp.where(step == down, 1.0, 0.0)
        steps.append(step)
    earlier = jnp.where(down < across, 1.0, 0.0).astype(jnp.bfloat16)
    before = jnp.dot(
        held.astype(jnp.bfloat16), earlier, preferred_element_type=jnp.float32
    ).astype(jnp.int32)
    for k in range(TOP):
        place_of = jnp.sum(jnp.where(steps[k] == down, before, 0), axis=0, keepdims=True)
        row_out[k : k + 1, :] = steps[k] * CAP + place_of
    token_out[...] = jnp.zeros_like(token_out)
    for slot in range(CAP):
        fits = jnp.where((held > 0.5) & (before == slot), across, 0)
        token_out[:, slot : slot + 1] = jnp.sum(fits, axis=1, keepdims=True)


HEAD_BLOCK = 8 * HEAD_SIZE
TOK = 128
ZS = 4
WIDE = 256
BLOCKS = D // WIDE
HALF = 256


def mix_kernel(
    query_ref,
    key_ref,
    value_ref,
    weight_ref,
    hidden_ref,
    gain_hbm,
    ids_hbm,
    mixed_out,
    normed_ref,
    row_out,
    token_out,
    q_all,
    k_all,
    v_all,
    w_all,
    att,
    part,
    relay,
    final,
    held,
    mixed_ref,
    ids_ref,
    gain_ref,
    folded,
    q_send,
    q_recv,
    k_send,
    k_recv,
    v_send,
    v_recv,
    w1_send,
    w1_recv,
    w2_send,
    w2_recv,
    wd_send,
    wd_recv,
    rs_send,
    relay_recv,
    final_recv,
    held_sem,
    ids_sem,
    mixed_sem,
    gain_sem,
):
    z, c, x, y = place()
    sp, ep = z * 2 + c, x * 4 + y

    def remote(src, dst, send_sem, recv_sem, to):
        pltpu.make_async_remote_copy(
            src_ref=src,
            dst_ref=dst,
            send_sem=send_sem,
            recv_sem=recv_sem,
            device_id=to,
            device_id_type=MESH,
        ).start()

    def local(src, dst, sem):
        pltpu.make_async_copy(src, dst, sem).start()

    def settle(ref, sem):
        pltpu.make_async_copy(ref, ref, sem).wait()

    local(hidden_ref, held, held_sem)
    local(ids_hbm, ids_ref, ids_sem)
    local(gain_hbm, gain_ref, gain_sem)
    barrier = pltpu.get_barrier_semaphore()
    for d in range(1, 8):
        pl.semaphore_signal(barrier, inc=1, device_id=((sp + d) % 8, ep), device_id_type=MESH)
    for d in range(1, 4):
        along_x, along_y = (sp, ((x + d) % 4) * 4 + y), (sp, x * 4 + (y + d) % 4)
        pl.semaphore_signal(barrier, inc=1, device_id=along_x, device_id_type=MESH)
        pl.semaphore_signal(barrier, inc=1, device_id=along_y, device_id_type=MESH)
    pl.semaphore_wait(barrier, 13)

    def group_of(other):
        return pl.ds(pl.multiple_of(other // 4 * HEAD_SIZE, HEAD_SIZE), HEAD_SIZE)

    def heads_of(chip):
        return pl.ds(pl.multiple_of(chip * HEAD_BLOCK, HEAD_BLOCK), HEAD_BLOCK)

    top, low = pl.ds(0, HALF), pl.ds(HALF, HALF)
    for d in range(1, 8):
        other = (sp + d) % 8
        remote(key_ref.at[:, group_of(other)], k_all.at[sp], k_send, k_recv, (other, ep))
        remote(value_ref.at[:, group_of(other)], v_all.at[sp], v_send, v_recv, (other, ep))
    for d in range(1, 4):
        along_x, along_y = (sp, ((x + d) % 4) * 4 + y), (sp, x * 4 + (y + d) % 4)
        remote(weight_ref.at[top], w_all.at[ep, c, top], w1_send.at[0], w1_recv.at[0], along_x)
        remote(weight_ref.at[low], w_all.at[ep, c, low], w1_send.at[1], w1_recv.at[1], along_y)
    for d in (1, 3, 2):
        chip = (z + d) % 4
        remote(
            query_ref.at[:, heads_of(chip)], q_all.at[z], q_send, q_recv.at[z], (chip * 2 + c, ep)
        )
    local(key_ref.at[:, group_of(sp)], k_all.at[sp], k_recv)
    local(value_ref.at[:, group_of(sp)], v_all.at[sp], v_recv)
    local(query_ref.at[:, heads_of(z)], q_all.at[z], q_recv.at[z])
    local(weight_ref.at[top], w_all.at[ep, c, top], w1_recv.at[0])
    local(weight_ref.at[low], w_all.at[ep, c, low], w1_recv.at[1])

    settle(w_all.at[pl.ds(0, 2), 0], w1_recv.at[0])
    settle(w_all.at[pl.ds(0, 2), 0], w1_recv.at[1])
    twin = (z * 2 + 1 - c, ep)

    def second(d):
        def send(k, carry):
            mine = w_all.at[k * 4 + y, c, top]
            remote(mine, mine, w2_send.at[0], w2_recv.at[0, d], (sp, x * 4 + (y + d) % 4))
            mine = w_all.at[x * 4 + k, c, low]
            remote(mine, mine, w2_send.at[1], w2_recv.at[1, d], (sp, ((x + d) % 4) * 4 + y))
            return carry

        lax.fori_loop(0, 4, send, 0)

    second(1)
    second(3)

    def share(d):
        def send(k, carry):
            mine = w_all.at[k * 4 + (y + 4 - d) % 4, c, top]
            remote(mine, mine, wd_send, wd_recv.at[d], twin)
            mine = w_all.at[((x + 4 - d) % 4) * 4 + k, c, low]
            remote(mine, mine, wd_send, wd_recv.at[d], twin)
            return carry

        lax.fori_loop(0, 4, send, 0)

    def arrive(d):
        settle(w_all.at[pl.ds(0, 2), 0], w2_recv.at[0, d])
        settle(w_all.at[pl.ds(0, 2), 0], w2_recv.at[1, d])
        share(d)

    share(0)

    settle(ids_ref, ids_sem)
    route(ids_ref, row_out, token_out)

    settle(k_all, k_recv)
    settle(v_all, v_recv)
    scale = np.float32(np.log2(np.e) / np.sqrt(HEAD_SIZE))

    def attend(block):
        settle(q_all.at[block], q_recv.at[block])
        past = 2 * block * TOK

        def against(rows, first, length):
            return lax.dot_general(
                rows,
                k_all[first : first + length].reshape(length * TOK, HEAD_SIZE),
                (((1,), (1,)), ((), ())),
                preferred_element_type=jnp.float32,
            )

        def times(probs, first, length):
            return jnp.dot(
                probs.astype(jnp.bfloat16),
                v_all[first : first + length].reshape(length * TOK, HEAD_SIZE),
                preferred_element_type=jnp.float32,
            )

        def heads(pair, carry):
            cols = pl.ds(pl.multiple_of(pair * 256, 256), 256)
            both = q_all[block, :, cols]
            rows = jnp.concatenate([both[:, :HEAD_SIZE], both[:, HEAD_SIZE:]], axis=0)
            near = against(rows, 2 * block, 2)
            row = lax.broadcasted_iota(jnp.int32, near.shape, 0) % TOK + c * TOK
            col = lax.broadcasted_iota(jnp.int32, near.shape, 1)
            near = jnp.where(col <= row, near, jnp.float32(-1e30))
            top = jnp.max(near, axis=-1, keepdims=True)
            if past:
                far = against(rows, 0, 2 * block)
                top = jnp.maximum(top, jnp.max(far, axis=-1, keepdims=True))
            near = jnp.exp2((near - top) * scale)
            total = jnp.sum(near, axis=-1, keepdims=True)
            out = times(near, 2 * block, 2)
            if past:
                far = jnp.exp2((far - top) * scale)
                total = total + jnp.sum(far, axis=-1, keepdims=True)
                out = out + times(far, 0, 2 * block)
            out = (out * (1.0 / total)).astype(jnp.bfloat16)
            att[block * TOK : (block + 1) * TOK, cols] = jnp.concatenate(
                [out[:TOK], out[TOK:]], axis=1
            )
            return carry

        lax.fori_loop(0, 4, heads, 0)

    attend(0)
    attend(1)
    arrive(1)
    arrive(3)
    second(2)
    attend(2)
    attend(3)

    across = (z + 2) % 4

    def block_of(i):
        near = i // 9 == 0
        r = i % 9
        q = r // 4
        skip = lambda v: v + v // 2
        a = jnp.where(near, skip(r // 3), 2 * (1 - q) + q * skip(r % 4))
        b = jnp.where(near, skip(r % 3), (r % 4) * (1 - q) + 2 * q)
        return ((x + a) % 4) * 4 + (y + b) % 4

    def project(i, carry):
        j, odd = block_of(i), i % 2
        part[j] = (
            jnp.dot(att[...], w_all[j].reshape(2 * 512, WIDE), preferred_element_type=jnp.float32)
            .astype(jnp.bfloat16)
            .reshape(ZS, TOK, WIDE)
        )
        onward, straight = (z + 1 + 2 * odd) % 4, (z + 3 - 2 * odd) % 4
        remote(
            part.at[j, across], relay.at[j], rs_send, relay_recv.at[j], (onward * 2 + c, ep)
        )
        remote(
            part.at[j, straight],
            final.at[1 - odd, j],
            rs_send,
            final_recv.at[1 - odd, j],
            (straight * 2 + c, ep),
        )
        return carry

    def pass_on(i, carry):
        j, odd = block_of(i), i % 2
        onward = (z + 1 + 2 * odd) % 4
        settle(relay.at[j], relay_recv.at[j])
        part[j, onward] = (
            part[j, onward].astype(jnp.float32) + relay[j].astype(jnp.float32)
        ).astype(jnp.bfloat16)
        remote(
            part.at[j, onward],
            final.at[odd, j],
            rs_send,
            final_recv.at[odd, j],
            (onward * 2 + c, ep),
        )
        return carry

    for d in (0, 1, 3):
        settle(w_all.at[pl.ds(0, 4), 0], wd_recv.at[d])
    lax.fori_loop(0, 9, project, 0)
    lax.fori_loop(0, 9, pass_on, 0)
    arrive(2)
    settle(w_all.at[pl.ds(0, 4), 0], wd_recv.at[2])
    lax.fori_loop(9, BLOCKS, project, 0)
    lax.fori_loop(9, BLOCKS, pass_on, 0)

    def finish(j, squares):
        for side in range(2):
            settle(final.at[side, j], final_recv.at[side, j])
        cols = pl.ds(pl.multiple_of(j * WIDE, WIDE), WIDE)
        total = held[:, cols].astype(jnp.float32) + part[j, z].astype(jnp.float32)
        total = total + final[0, j].astype(jnp.float32) + final[1, j].astype(jnp.float32)
        mixed = total.astype(jnp.bfloat16)
        mixed_ref[:, cols] = mixed
        wide = mixed.astype(jnp.float32)
        wide = wide * wide
        return squares + wide[:, :LANES] + wide[:, LANES:]

    settle(held, held_sem)
    squares = lax.fori_loop(0, BLOCKS, finish, jnp.zeros((TOK, LANES), jnp.float32))
    local(mixed_ref, mixed_out, mixed_sem)
    inverse = lax.rsqrt(jnp.sum(squares, axis=-1, keepdims=True) * np.float32(1.0 / D) + 1e-06)

    settle(gain_ref, gain_sem)

    def norm(j, carry):
        cols = pl.ds(pl.multiple_of(j * WIDE, WIDE), WIDE)
        normed = mixed_ref[:, cols].astype(jnp.float32) * inverse * gain_ref[:, cols]
        for half in range(WIDE // LANES):
            folded[pl.ds(j * (WIDE // LANES) + half, TOK, stride=FEATS), :] = normed[
                :, half * LANES : (half + 1) * LANES
            ]
        return carry

    lax.fori_loop(0, BLOCKS, norm, 0)

    def narrow(i, carry):
        part = folded[pl.ds(pl.multiple_of(i * 16 * FEATS, 16 * FEATS), 16 * FEATS), :]
        normed_ref[pl.ds(i * 16, 16)] = part.reshape(16, FEATS, LANES).astype(jnp.bfloat16)
        return carry

    lax.fori_loop(0, TOK // 16, narrow, 0)

    settle(mixed_ref, mixed_sem)
    settle(q_all.at[pl.ds(0, 3)], q_send)
    settle(k_all.at[pl.ds(0, 7)], k_send)
    settle(v_all.at[pl.ds(0, 7)], v_send)
    for i in range(2):
        settle(w_all.at[pl.ds(0, 3), 0, top], w1_send.at[i])
        settle(w_all.at[pl.ds(0, 6), 0], w2_send.at[i])
    settle(w_all.at[pl.ds(0, 16), 0], wd_send)
    settle(part.at[:, pl.ds(0, 3)], rs_send)


def mix(queries, keys, values, out_weight, hidden, gain, ids):
    bf16 = jnp.bfloat16
    vmem = pl.BlockSpec(memory_space=pltpu.VMEM)
    anywhere = pl.BlockSpec(memory_space=pl.ANY)
    dma = pltpu.SemaphoreType.DMA
    shape = jax.ShapeDtypeStruct((TOK, D), bf16)
    return pl.pallas_call(
        mix_kernel,
        out_shape=(
            shape,
            jax.ShapeDtypeStruct((TOK, FEATS, LANES), bf16),
            jax.ShapeDtypeStruct((TOP, TOK), jnp.int32),
            jax.ShapeDtypeStruct((DEVICES, 16), jnp.int32),
        ),
        in_specs=[anywhere] * 7,
        out_specs=(anywhere, vmem, vmem, vmem),
        scratch_shapes=[
            pltpu.VMEM((ZS, TOK, HEAD_BLOCK), bf16),
            pltpu.VMEM((8, TOK, HEAD_SIZE), bf16),
            pltpu.VMEM((8, TOK, HEAD_SIZE), bf16),
            pltpu.VMEM((BLOCKS, 2, 512, WIDE), bf16),
            pltpu.VMEM((ZS * TOK, HEAD_BLOCK), bf16),
            pltpu.VMEM((BLOCKS, ZS, TOK, WIDE), bf16),
            pltpu.VMEM((BLOCKS, TOK, WIDE), bf16),
            pltpu.VMEM((2, BLOCKS, TOK, WIDE), bf16),
            pltpu.VMEM((TOK, D), bf16),
            pltpu.VMEM((TOK, D), bf16),
            pltpu.VMEM((TOP, TOK), jnp.int32),
            pltpu.VMEM((1, D), jnp.float32),
            pltpu.VMEM((TOK * FEATS, LANES), jnp.float32),
            dma,
            dma((ZS,)),
            dma,
            dma,
            dma,
            dma,
            dma((2,)),
            dma((2,)),
            dma((2,)),
            dma((2, 4)),
            dma,
            dma((4,)),
            dma,
            dma((BLOCKS,)),
            dma((2, BLOCKS)),
            dma,
            dma,
            dma,
            dma,
        ],
        compiler_params=pltpu.CompilerParams(
            collective_id=1, has_side_effects=True, vmem_limit_bytes=62 * 2**20
        ),
        name="mix",
    )(queries, keys, values, out_weight, hidden, gain, ids)


def body(
    hidden_in,
    queries,
    keys,
    values,
    out_weight,
    norm_gain,
    gate_weight,
    up_weight,
    down_weight,
    expert_ids,
    gates,
    cotangent,
):
    tok = queries.shape[1]
    mixed, normed, row_of, token_of = mix(
        queries[0],
        keys[0],
        values[0],
        out_weight,
        hidden_in[0],
        norm_gain.reshape(1, D),
        expert_ids[0].T,
    )
    out, grads = run_experts(
        token_of,
        row_of,
        gates[0].T,
        normed,
        mixed,
        cotangent[0],
        gate_weight[0],
        up_weight[0],
        down_weight[0],
    )
    return (out.reshape(1, tok, D), jnp.sum(grads, axis=-1).T[None])


def solution(mesh):
    placed = (
        P("ep", "sp", None),
        P("ep", "sp", None),
        P("ep", "sp", None),
        P("ep", "sp", None),
        P("sp", "ep"),
        P(),
        P(("sp", "ep"), None, None),
        P(("sp", "ep"), None, None),
        P(("sp", "ep"), None, None),
        P("ep", "sp", None),
        P("ep", "sp", None),
        P("ep", "sp", None),
    )
    return jax.shard_map(
        body,
        mesh=mesh,
        in_specs=placed,
        out_specs=(P("ep", "sp", None), P("ep", "sp", None)),
        check_vma=False,
    )
```

```python
import jax
import jax.numpy as jnp
import numpy as np
from jax import lax
from jax.experimental import pallas as pl
from jax.experimental.pallas import tpu as pltpu
from jax.sharding import PartitionSpec as P

D = 4096
HEAD_SIZE = 128
TOP = 8


MESH = pl.DeviceIdType.MESH
CAP = 9
DEVICES = 128
ROWS = DEVICES * CAP
GROUPS = 8
GROUP_SLOTS = DEVICES // GROUPS
GROUP_ROWS = GROUP_SLOTS * CAP
FFW = 768
LANES = 128
FEATS = D // LANES


def offset_of(step):
    a, b, c, e = step % 4, (step // 4) % 4, (step // 16) % 4, step // 64
    return (3 * a + b + c) % 4, (a + b + e) % 2, a, (a + b) % 4


def place():
    sp, ep = lax.axis_index("sp"), lax.axis_index("ep")
    return sp // 2, sp % 2, ep // 4, ep % 4


def target_of(step):
    z, c, x, y = place()
    dz, dc, dx, dy = offset_of(step)
    turn = 1 - 2 * c
    return (
        ((z + turn * dz + 4) % 4) * 2 + (c + dc) % 2,
        ((x + turn * dx + 4) % 4) * 4 + (y + turn * dy + 4) % 4,
    )


def source_of(step):
    z, c, x, y = place()
    dz, dc, dx, dy = offset_of(step)
    core = (c + dc) % 2
    turn = 1 - 2 * core
    return (
        ((z - turn * dz + 4) % 4) * 2 + core,
        ((x - turn * dx + 4) % 4) * 4 + (y - turn * dy + 4) % 4,
    )


def chunk(step):
    return pl.ds(step * CAP, CAP)


def expert_kernel(
    token_hbm,
    row_hbm,
    scale_hbm,
    normed_ref,
    mixed_hbm,
    cot_hbm,
    gate_hbm,
    up_hbm,
    down_hbm,
    out_ref,
    grad_ref,
    back_ref,
    gate_w,
    up_w,
    down_w,
    send,
    recv,
    rows,
    inner,
    wide,
    flat,
    mixed_ref,
    cot_ref,
    scale_ref,
    token_ref,
    row_ref,
    flat_sem,
    weight_sem,
    send_sem,
    recv_sem,
    out_sem,
    back_sem,
):
    small = [
        pltpu.make_async_copy(src, dst, flat_sem.at[i])
        for i, (src, dst) in enumerate(
            ((scale_hbm, scale_ref), (row_hbm, row_ref), (cot_hbm, flat))
        )
    ]
    tokens = pltpu.make_async_copy(token_hbm, token_ref, flat_sem.at[4])
    tokens.start()
    weights = [
        pltpu.make_async_copy(src, dst, weight_sem.at[i])
        for i, (src, dst) in enumerate(((gate_hbm, gate_w), (up_hbm, up_w), (down_hbm, down_w)))
    ]
    for copy in weights:
        copy.start()

    for copy in small:
        copy.start()

    barrier = pltpu.get_barrier_semaphore()

    def greet(step, carry):
        pl.semaphore_signal(barrier, inc=1, device_id=target_of(step), device_id_type=MESH)
        return carry

    lax.fori_loop(1, DEVICES, greet, 0)

    def fill(step):
        for slot in range(CAP):
            row = step * CAP + slot
            send[row] = normed_ref[token_ref[step, slot]]

    tokens.wait()
    fill(0)
    pl.semaphore_wait(barrier, DEVICES - 1)
    pltpu.make_async_copy(send.at[chunk(0)], recv.at[chunk(0)], recv_sem.at[0]).start()

    def dispatch(step, carry):
        fill(step)
        pltpu.make_async_remote_copy(
            src_ref=send.at[chunk(step)],
            dst_ref=recv.at[chunk(step)],
            send_sem=send_sem,
            recv_sem=recv_sem.at[step // GROUP_SLOTS],
            device_id=target_of(step),
            device_id_type=MESH,
        ).start()
        return carry

    lax.fori_loop(1, DEVICES, dispatch, 0)

    def fold(src, dst):
        def turn(i, carry):
            for f in range(FEATS):
                wide[pl.ds(f, 16, stride=FEATS), :] = src[
                    pl.ds(pl.multiple_of(i * 16, 16), 16), f * LANES : (f + 1) * LANES
                ].astype(jnp.float32)
            dst[pl.ds(i * 16, 16)] = (
                wide[pl.ds(0, 16 * FEATS), :].reshape(16, FEATS, LANES).astype(jnp.bfloat16)
            )
            return carry

        lax.fori_loop(0, src.shape[0] // 16, turn, 0)

    for copy in weights:
        copy.wait()

    def work(group, carry):
        base = group * GROUP_ROWS
        block = pl.ds(base, GROUP_ROWS)
        pltpu.make_async_copy(recv.at[block], recv.at[block], recv_sem.at[group]).wait()

        def turn_in(i, carry):
            wide[pl.ds(0, 16 * FEATS), :] = (
                recv[pl.ds(base + i * 16, 16)].astype(jnp.float32).reshape(16 * FEATS, LANES)
            )
            for f in range(FEATS):
                rows[pl.ds(pl.multiple_of(i * 16, 16), 16), f * LANES : (f + 1) * LANES] = wide[
                    pl.ds(f, 16, stride=FEATS), :
                ].astype(jnp.bfloat16)
            return carry

        lax.fori_loop(0, GROUP_ROWS // 16, turn_in, 0)

        def hidden(n, carry):
            cols = pl.ds(pl.multiple_of(n * 256, 256), 256)
            gate_part = jnp.dot(rows[...], gate_w[:, cols], preferred_element_type=jnp.float32)
            up_part = jnp.dot(rows[...], up_w[:, cols], preferred_element_type=jnp.float32)
            inner[:, cols] = (gate_part / (1.0 + jnp.exp(-gate_part)) * up_part).astype(
                jnp.bfloat16
            )
            return carry

        lax.fori_loop(0, FFW // 256, hidden, 0)

        def project(n, carry):
            part = jnp.dot(
                inner[...],
                down_w[:, pl.ds(pl.multiple_of(n * 512, 512), 512)],
                preferred_element_type=jnp.float32,
            )
            for j in range(4):
                wide[pl.ds(n * 4 + j, GROUP_ROWS, stride=FEATS), :] = part[
                    :, j * LANES : (j + 1) * LANES
                ]
            return carry

        lax.fori_loop(0, D // 512, project, 0)

        def turn_out(i, carry):
            part = wide[pl.ds(pl.multiple_of(i * 16 * FEATS, 16 * FEATS), 16 * FEATS), :]
            recv[pl.ds(base + i * 16, 16)] = part.reshape(16, FEATS, LANES).astype(jnp.bfloat16)
            return carry

        lax.fori_loop(0, GROUP_ROWS // 16, turn_out, 0)

        def give_back(step, carry):
            pltpu.make_async_remote_copy(
                src_ref=recv.at[chunk(step)],
                dst_ref=back_ref.at[chunk(step)],
                send_sem=out_sem,
                recv_sem=back_sem,
                device_id=source_of(step),
                device_id_type=MESH,
            ).start()
            return carry

        @pl.when(group == 0)
        def _():
            pltpu.make_async_copy(recv.at[chunk(0)], back_ref.at[chunk(0)], back_sem).start()

        lax.fori_loop(
            jnp.maximum(group * GROUP_SLOTS, 1), (group + 1) * GROUP_SLOTS, give_back, 0
        )
        return carry

    lax.fori_loop(0, GROUPS, work, 0)
    for copy in small:
        copy.wait()
    fold(flat, cot_ref)
    last = pltpu.make_async_copy(mixed_hbm, flat, flat_sem.at[3])
    last.start()
    last.wait()
    fold(flat, mixed_ref)
    far = pl.ds(CAP, ROWS - CAP)
    pltpu.make_async_copy(send.at[far], send.at[far], send_sem).wait()
    pltpu.make_async_copy(recv.at[far], recv.at[far], out_sem).wait()
    pltpu.make_async_copy(back_ref, back_ref, back_sem).wait()

    def combine(t, carry):
        cot = cot_ref[t].astype(jnp.float32)
        total = mixed_ref[t].astype(jnp.float32)
        for k in range(TOP):
            row = back_ref[row_ref[k, t]].astype(jnp.float32)
            total = total + scale_ref[k, t] * row
            grad_ref[k, pl.ds(t, 1), :] = jnp.sum(cot * row, axis=0, keepdims=True)
        out_ref[t] = total.astype(jnp.bfloat16)
        return carry

    lax.fori_loop(0, out_ref.shape[0], combine, 0)


def run_experts(
    token_of, row_of, gates, normed, mixed, cotangent, gate_weight, up_weight, down_weight
):
    bf16 = jnp.bfloat16
    tok = normed.shape[0]
    anywhere = pl.BlockSpec(memory_space=pl.ANY)
    vmem = pl.BlockSpec(memory_space=pltpu.VMEM)
    return pl.pallas_call(
        expert_kernel,
        out_shape=(
            jax.ShapeDtypeStruct((tok, FEATS, LANES), bf16),
            jax.ShapeDtypeStruct((TOP, tok, LANES), jnp.float32),
        ),
        in_specs=[anywhere] * 3 + [vmem] + [anywhere] * 5,
        out_specs=(vmem, vmem),
        scratch_shapes=[
            pltpu.VMEM((ROWS, FEATS, LANES), bf16),
            pltpu.VMEM((D, FFW), bf16),
            pltpu.VMEM((D, FFW), bf16),
            pltpu.VMEM((FFW, D), bf16),
            pltpu.VMEM((ROWS, FEATS, LANES), bf16),
            pltpu.VMEM((ROWS, FEATS, LANES), bf16),
            pltpu.VMEM((GROUP_ROWS, D), bf16),
            pltpu.VMEM((GROUP_ROWS, FFW), bf16),
            pltpu.VMEM((GROUP_ROWS * FEATS, LANES), jnp.float32),
            pltpu.VMEM((tok, D), bf16),
            pltpu.VMEM((tok, FEATS, LANES), bf16),
            pltpu.VMEM((tok, FEATS, LANES), bf16),
            pltpu.SMEM((TOP, tok), jnp.float32),
            pltpu.SMEM((DEVICES, 16), jnp.int32),
            pltpu.SMEM((TOP, tok), jnp.int32),
            pltpu.SemaphoreType.DMA((5,)),
            pltpu.SemaphoreType.DMA((3,)),
            pltpu.SemaphoreType.DMA,
            pltpu.SemaphoreType.DMA((GROUPS,)),
            pltpu.SemaphoreType.DMA,
            pltpu.SemaphoreType.DMA,
        ],
        compiler_params=pltpu.CompilerParams(
            collective_id=0, has_side_effects=True, vmem_limit_bytes=60 * 2**20
        ),
        name="experts",
    )(token_of, row_of, gates, normed, mixed, cotangent, gate_weight, up_weight, down_weight)


def route(ids_ref, row_out, token_out):
    square = (DEVICES, DEVICES)
    down = lax.broadcasted_iota(jnp.int32, square, 0)
    across = lax.broadcasted_iota(jnp.int32, square, 1)
    sp, ep = target_of(across)
    step_of = jnp.sum(jnp.where(sp * 16 + ep == down, across, 0), axis=1, keepdims=True)
    steps = []
    held = jnp.zeros(square, jnp.float32)
    for k in range(TOP):
        named = ids_ref[k : k + 1, :] == down
        step = jnp.sum(jnp.where(named, step_of, 0), axis=0, keepdims=True)
        held = held + jnp.where(step == down, 1.0, 0.0)
        steps.append(step)
    earlier = jnp.where(down < across, 1.0, 0.0).astype(jnp.bfloat16)
    before = jnp.dot(
        held.astype(jnp.bfloat16), earlier, preferred_element_type=jnp.float32
    ).astype(jnp.int32)
    for k in range(TOP):
        place_of = jnp.sum(jnp.where(steps[k] == down, before, 0), axis=0, keepdims=True)
        row_out[k : k + 1, :] = steps[k] * CAP + place_of
    token_out[...] = jnp.zeros_like(token_out)
    for slot in range(CAP):
        fits = jnp.where((held > 0.5) & (before == slot), across, 0)
        token_out[:, slot : slot + 1] = jnp.sum(fits, axis=1, keepdims=True)


HEAD_BLOCK = 8 * HEAD_SIZE
TOK = 128
ZS = 4
WIDE = 256
BLOCKS = D // WIDE
HALF = 256


def mix_kernel(
    query_ref,
    key_ref,
    value_ref,
    weight_ref,
    hidden_ref,
    gain_hbm,
    ids_hbm,
    mixed_out,
    normed_ref,
    row_out,
    token_out,
    q_all,
    k_all,
    v_all,
    w_all,
    att,
    part,
    relay,
    final,
    held,
    mixed_ref,
    ids_ref,
    gain_ref,
    folded,
    q_send,
    q_recv,
    k_send,
    k_recv,
    v_send,
    v_recv,
    w1_send,
    w1_recv,
    w2_send,
    w2_recv,
    wd_send,
    wd_recv,
    rs_send,
    relay_recv,
    final_recv,
    held_sem,
    ids_sem,
    mixed_sem,
    gain_sem,
):
    z, c, x, y = place()
    sp, ep = z * 2 + c, x * 4 + y

    def remote(src, dst, send_sem, recv_sem, to):
        pltpu.make_async_remote_copy(
            src_ref=src,
            dst_ref=dst,
            send_sem=send_sem,
            recv_sem=recv_sem,
            device_id=to,
            device_id_type=MESH,
        ).start()

    def local(src, dst, sem):
        pltpu.make_async_copy(src, dst, sem).start()

    def settle(ref, sem):
        pltpu.make_async_copy(ref, ref, sem).wait()

    local(hidden_ref, held, held_sem)
    local(ids_hbm, ids_ref, ids_sem)
    local(gain_hbm, gain_ref, gain_sem)
    barrier = pltpu.get_barrier_semaphore()
    for d in range(1, 8):
        pl.semaphore_signal(barrier, inc=1, device_id=((sp + d) % 8, ep), device_id_type=MESH)
    for d in range(1, 4):
        along_x, along_y = (sp, ((x + d) % 4) * 4 + y), (sp, x * 4 + (y + d) % 4)
        pl.semaphore_signal(barrier, inc=1, device_id=along_x, device_id_type=MESH)
        pl.semaphore_signal(barrier, inc=1, device_id=along_y, device_id_type=MESH)
    pl.semaphore_wait(barrier, 13)

    def group_of(other):
        return pl.ds(pl.multiple_of(other // 4 * HEAD_SIZE, HEAD_SIZE), HEAD_SIZE)

    def heads_of(chip):
        return pl.ds(pl.multiple_of(chip * HEAD_BLOCK, HEAD_BLOCK), HEAD_BLOCK)

    top, low = pl.ds(0, HALF), pl.ds(HALF, HALF)
    for d in range(1, 8):
        other = (sp + d) % 8
        remote(key_ref.at[:, group_of(other)], k_all.at[sp], k_send, k_recv, (other, ep))
        remote(value_ref.at[:, group_of(other)], v_all.at[sp], v_send, v_recv, (other, ep))
    for d in range(1, 4):
        along_x, along_y = (sp, ((x + d) % 4) * 4 + y), (sp, x * 4 + (y + d) % 4)
        remote(weight_ref.at[top], w_all.at[ep, c, top], w1_send.at[0], w1_recv.at[0], along_x)
        remote(weight_ref.at[low], w_all.at[ep, c, low], w1_send.at[1], w1_recv.at[1], along_y)
    for d in (1, 3, 2):
        chip = (z + d) % 4
        remote(
            query_ref.at[:, heads_of(chip)], q_all.at[z], q_send, q_recv.at[z], (chip * 2 + c, ep)
        )
    local(key_ref.at[:, group_of(sp)], k_all.at[sp], k_recv)
    local(value_ref.at[:, group_of(sp)], v_all.at[sp], v_recv)
    local(query_ref.at[:, heads_of(z)], q_all.at[z], q_recv.at[z])
    local(weight_ref.at[top], w_all.at[ep, c, top], w1_recv.at[0])
    local(weight_ref.at[low], w_all.at[ep, c, low], w1_recv.at[1])

    settle(w_all.at[pl.ds(0, 2), 0], w1_recv.at[0])
    settle(w_all.at[pl.ds(0, 2), 0], w1_recv.at[1])
    twin = (z * 2 + 1 - c, ep)

    def second(d):
        def send(k, carry):
            mine = w_all.at[k * 4 + y, c, top]
            remote(mine, mine, w2_send.at[0], w2_recv.at[0, d], (sp, x * 4 + (y + d) % 4))
            mine = w_all.at[x * 4 + k, c, low]
            remote(mine, mine, w2_send.at[1], w2_recv.at[1, d], (sp, ((x + d) % 4) * 4 + y))
            return carry

        lax.fori_loop(0, 4, send, 0)

    second(1)
    second(3)

    def share(d):
        def send(k, carry):
            mine = w_all.at[k * 4 + (y + 4 - d) % 4, c, top]
            remote(mine, mine, wd_send, wd_recv.at[d], twin)
            mine = w_all.at[((x + 4 - d) % 4) * 4 + k, c, low]
            remote(mine, mine, wd_send, wd_recv.at[d], twin)
            return carry

        lax.fori_loop(0, 4, send, 0)

    def arrive(d):
        settle(w_all.at[pl.ds(0, 2), 0], w2_recv.at[0, d])
        settle(w_all.at[pl.ds(0, 2), 0], w2_recv.at[1, d])
        share(d)

    share(0)

    settle(ids_ref, ids_sem)
    route(ids_ref, row_out, token_out)

    settle(k_all, k_recv)
    settle(v_all, v_recv)
    scale = np.float32(np.log2(np.e) / np.sqrt(HEAD_SIZE))

    def attend(block):
        settle(q_all.at[block], q_recv.at[block])
        past = 2 * block * TOK

        def against(rows, first, length):
            return lax.dot_general(
                rows,
                k_all[first : first + length].reshape(length * TOK, HEAD_SIZE),
                (((1,), (1,)), ((), ())),
                preferred_element_type=jnp.float32,
            )

        def times(probs, first, length):
            return jnp.dot(
                probs.astype(jnp.bfloat16),
                v_all[first : first + length].reshape(length * TOK, HEAD_SIZE),
                preferred_element_type=jnp.float32,
            )

        def heads(pair, carry):
            cols = pl.ds(pl.multiple_of(pair * 256, 256), 256)
            both = q_all[block, :, cols]
            rows = jnp.concatenate([both[:, :HEAD_SIZE], both[:, HEAD_SIZE:]], axis=0)
            near = against(rows, 2 * block, 2)
            row = lax.broadcasted_iota(jnp.int32, near.shape, 0) % TOK + c * TOK
            col = lax.broadcasted_iota(jnp.int32, near.shape, 1)
            near = jnp.where(col <= row, near, jnp.float32(-1e30))
            top = jnp.max(near, axis=-1, keepdims=True)
            if past:
                far = against(rows, 0, 2 * block)
                top = jnp.maximum(top, jnp.max(far, axis=-1, keepdims=True))
            near = jnp.exp2((near - top) * scale)
            total = jnp.sum(near, axis=-1, keepdims=True)
            out = times(near, 2 * block, 2)
            if past:
                far = jnp.exp2((far - top) * scale)
                total = total + jnp.sum(far, axis=-1, keepdims=True)
                out = out + times(far, 0, 2 * block)
            out = (out * (1.0 / total)).astype(jnp.bfloat16)
            att[block * TOK : (block + 1) * TOK, cols] = jnp.concatenate(
                [out[:TOK], out[TOK:]], axis=1
            )
            return carry

        lax.fori_loop(0, 4, heads, 0)

    attend(0)
    attend(1)
    arrive(1)
    arrive(3)
    second(2)
    attend(2)
    attend(3)

    across = (z + 2) % 4

    def block_of(i):
        near = i // 9 == 0
        r = i % 9
        q = r // 4
        skip = lambda v: v + v // 2
        a = jnp.where(near, skip(r // 3), 2 * (1 - q) + q * skip(r % 4))
        b = jnp.where(near, skip(r % 3), (r % 4) * (1 - q) + 2 * q)
        return ((x + a) % 4) * 4 + (y + b) % 4

    def project(i, carry):
        j, odd = block_of(i), i % 2
        part[j] = (
            jnp.dot(att[...], w_all[j].reshape(2 * 512, WIDE), preferred_element_type=jnp.float32)
            .astype(jnp.bfloat16)
            .reshape(ZS, TOK, WIDE)
        )
        onward, straight = (z + 1 + 2 * odd) % 4, (z + 3 - 2 * odd) % 4
        remote(
            part.at[j, across], relay.at[j], rs_send, relay_recv.at[j], (onward * 2 + c, ep)
        )
        remote(
            part.at[j, straight],
            final.at[1 - odd, j],
            rs_send,
            final_recv.at[1 - odd, j],
            (straight * 2 + c, ep),
        )
        return carry

    def pass_on(i, carry):
        j, odd = block_of(i), i % 2
        onward = (z + 1 + 2 * odd) % 4
        settle(relay.at[j], relay_recv.at[j])
        part[j, onward] = (
            part[j, onward].astype(jnp.float32) + relay[j].astype(jnp.float32)
        ).astype(jnp.bfloat16)
        remote(
            part.at[j, onward],
            final.at[odd, j],
            rs_send,
            final_recv.at[odd, j],
            (onward * 2 + c, ep),
        )
        return carry

    for d in (0, 1, 3):
        settle(w_all.at[pl.ds(0, 4), 0], wd_recv.at[d])
    lax.fori_loop(0, 9, project, 0)
    lax.fori_loop(0, 9, pass_on, 0)
    arrive(2)
    settle(w_all.at[pl.ds(0, 4), 0], wd_recv.at[2])
    lax.fori_loop(9, BLOCKS, project, 0)
    lax.fori_loop(9, BLOCKS, pass_on, 0)

    def finish(j, squares):
        for side in range(2):
            settle(final.at[side, j], final_recv.at[side, j])
        cols = pl.ds(pl.multiple_of(j * WIDE, WIDE), WIDE)
        total = held[:, cols].astype(jnp.float32) + part[j, z].astype(jnp.float32)
        total = total + final[0, j].astype(jnp.float32) + final[1, j].astype(jnp.float32)
        mixed = total.astype(jnp.bfloat16)
        mixed_ref[:, cols] = mixed
        wide = mixed.astype(jnp.float32)
        wide = wide * wide
        return squares + wide[:, :LANES] + wide[:, LANES:]

    settle(held, held_sem)
    squares = lax.fori_loop(0, BLOCKS, finish, jnp.zeros((TOK, LANES), jnp.float32))
    local(mixed_ref, mixed_out, mixed_sem)
    inverse = lax.rsqrt(jnp.sum(squares, axis=-1, keepdims=True) * np.float32(1.0 / D) + 1e-06)

    settle(gain_ref, gain_sem)

    def norm(j, carry):
        cols = pl.ds(pl.multiple_of(j * WIDE, WIDE), WIDE)
        normed = mixed_ref[:, cols].astype(jnp.float32) * inverse * gain_ref[:, cols]
        for half in range(WIDE // LANES):
            folded[pl.ds(j * (WIDE // LANES) + half, TOK, stride=FEATS), :] = normed[
                :, half * LANES : (half + 1) * LANES
            ]
        return carry

    lax.fori_loop(0, BLOCKS, norm, 0)

    def narrow(i, carry):
        part = folded[pl.ds(pl.multiple_of(i * 16 * FEATS, 16 * FEATS), 16 * FEATS), :]
        normed_ref[pl.ds(i * 16, 16)] = part.reshape(16, FEATS, LANES).astype(jnp.bfloat16)
        return carry

    lax.fori_loop(0, TOK // 16, narrow, 0)

    settle(mixed_ref, mixed_sem)
    settle(q_all.at[pl.ds(0, 3)], q_send)
    settle(k_all.at[pl.ds(0, 7)], k_send)
    settle(v_all.at[pl.ds(0, 7)], v_send)
    for i in range(2):
        settle(w_all.at[pl.ds(0, 3), 0, top], w1_send.at[i])
        settle(w_all.at[pl.ds(0, 6), 0], w2_send.at[i])
    settle(w_all.at[pl.ds(0, 16), 0], wd_send)
    settle(part.at[:, pl.ds(0, 3)], rs_send)


def mix(queries, keys, values, out_weight, hidden, gain, ids):
    bf16 = jnp.bfloat16
    vmem = pl.BlockSpec(memory_space=pltpu.VMEM)
    anywhere = pl.BlockSpec(memory_space=pl.ANY)
    dma = pltpu.SemaphoreType.DMA
    shape = jax.ShapeDtypeStruct((TOK, D), bf16)
    return pl.pallas_call(
        mix_kernel,
        out_shape=(
            shape,
            jax.ShapeDtypeStruct((TOK, FEATS, LANES), bf16),
            jax.ShapeDtypeStruct((TOP, TOK), jnp.int32),
            jax.ShapeDtypeStruct((DEVICES, 16), jnp.int32),
        ),
        in_specs=[anywhere] * 7,
        out_specs=(anywhere, vmem, vmem, vmem),
        scratch_shapes=[
            pltpu.VMEM((ZS, TOK, HEAD_BLOCK), bf16),
            pltpu.VMEM((8, TOK, HEAD_SIZE), bf16),
            pltpu.VMEM((8, TOK, HEAD_SIZE), bf16),
            pltpu.VMEM((BLOCKS, 2, 512, WIDE), bf16),
            pltpu.VMEM((ZS * TOK, HEAD_BLOCK), bf16),
            pltpu.VMEM((BLOCKS, ZS, TOK, WIDE), bf16),
            pltpu.VMEM((BLOCKS, TOK, WIDE), bf16),
            pltpu.VMEM((2, BLOCKS, TOK, WIDE), bf16),
            pltpu.VMEM((TOK, D), bf16),
            pltpu.VMEM((TOK, D), bf16),
            pltpu.VMEM((TOP, TOK), jnp.int32),
            pltpu.VMEM((1, D), jnp.float32),
            pltpu.VMEM((TOK * FEATS, LANES), jnp.float32),
            dma,
            dma((ZS,)),
            dma,
            dma,
            dma,
            dma,
            dma((2,)),
            dma((2,)),
            dma((2,)),
            dma((2, 4)),
            dma,
            dma((4,)),
            dma,
            dma((BLOCKS,)),
            dma((2, BLOCKS)),
            dma,
            dma,
            dma,
            dma,
        ],
        compiler_params=pltpu.CompilerParams(
            collective_id=1, has_side_effects=True, vmem_limit_bytes=62 * 2**20
        ),
        name="mix",
    )(queries, keys, values, out_weight, hidden, gain, ids)


def body(
    hidden_in,
    queries,
    keys,
    values,
    out_weight,
    norm_gain,
    gate_weight,
    up_weight,
    down_weight,
    expert_ids,
    gates,
    cotangent,
):
    tok = queries.shape[1]
    mixed, normed, row_of, token_of = mix(
        queries[0],
        keys[0],
        values[0],
        out_weight,
        hidden_in[0],
        norm_gain.reshape(1, D),
        expert_ids[0].T,
    )
    out, grads = run_experts(
        token_of,
        row_of,
        gates[0].T,
        normed,
        mixed,
        cotangent[0],
        gate_weight[0],
        up_weight[0],
        down_weight[0],
    )
    return (out.reshape(1, tok, D), jnp.sum(grads, axis=-1).T[None])


def solution(mesh):
    placed = (
        P("ep", "sp", None),
        P("ep", "sp", None),
        P("ep", "sp", None),
        P("ep", "sp", None),
        P("sp", "ep"),
        P(),
        P(("sp", "ep"), None, None),
        P(("sp", "ep"), None, None),
        P(("sp", "ep"), None, None),
        P("ep", "sp", None),
        P("ep", "sp", None),
        P("ep", "sp", None),
    )
    return jax.shard_map(
        body,
        mesh=mesh,
        in_specs=placed,
        out_specs=(P("ep", "sp", None), P("ep", "sp", None)),
        check_vma=False,
    )
```
